256 devices in a mesh: seq: 32 (over z, x_lo, core), head: 8 (over y, x_hi).
Axes of the slice: x: 4 (x_hi: 2, x_lo: 2; x = x_hi * 2 + x_lo), y: 4, z: 8, core: 2. Of those that a mesh axis runs over, the one named last changes fastest.
Arguments:
- latent: bfloat16 [4, 32, 64, 3072], P(None, 'seq', 'head'), may hold values from -6 to 6
- w_qkv: bfloat16 [3072, 3, 3072], P(None, None, 'head'), may hold values from -1 to 1
- q_gain: float32 [128], replicated, may hold values from 0.5 to 10
- k_gain: float32 [128], replicated, may hold values from 0.5 to 10
- w_out: bfloat16 [3072, 3072], P('head'), may hold values from -0.109375 to 0.109375
- neighbours: int32 [32, 9], replicated, may hold values from -1 to 31, as said below
- tile_owner: int32 [32], replicated, may hold values from 0 to 31, as said below
Outputs:
- mixed: bfloat16 [32, 256, 3072], P('seq', None, 'head')
The draws below stay inside these ranges and needn't reach their ends.
Inputs may be any that keep to these rules, and one draw needn't show every extreme that they name: `neighbours`: row t lists, in increasing order and followed by -1s, the tiles of the grid whose tile row differs from t's by at most one and whose tile column lies in a block of three consecutive tile columns that holds t's column; t itself is always listed. `tile_owner`: every index of seq owns exactly one tile.
All inputs are finite; a program needn't handle non-finite values.
Results may differ from the reference program's by a relative error of at most 0.017.
Values may be sent and summed in bfloat16 or wider, within the bound.
No kernel may reach another device: no remote copies, remote signals or barrier semaphores. Data moves between devices by JAX's collectives and lax.ppermute only.
A program may use at most 64 MiB of HBM per device.

```python
import jax
import jax.numpy as jnp
from jax import lax

D = 3072
HEADS = 24
HEAD_DIM = 128
FRAMES = 4
TILE = 8
TILE_COLS = 8
ROWS = 32
COLS = 64
TILES = 32
TILES_DEV = 1
TILE_TOKENS = 256
N_HEAD = 8


def draw_w_qkv(key, part):
    key = jax.random.fold_in(key, 11)
    query_key, fresh_key, value_key = jax.random.split(key, 3)
    total_width = HEADS * HEAD_DIM
    weight_scale = D ** (-0.5)
    query_part = jnp.clip(jax.random.normal(query_key, (D, total_width), jnp.float32), -5.0, 5.0) * weight_scale
    fresh_part = jnp.clip(jax.random.normal(fresh_key, (D, total_width), jnp.float32), -5.0, 5.0) * weight_scale
    value_part = jnp.clip(jax.random.normal(value_key, (D, total_width), jnp.float32), -5.0, 5.0) * weight_scale
    key_part = fresh_part
    return jnp.stack([query_part, key_part, value_part], axis=1).astype(jnp.bfloat16)


def draw_q_gain(key, part):
    key = jax.random.fold_in(key, 13)
    return jax.random.uniform(key, (HEAD_DIM,), jnp.float32, 0.5, 2.0)


def draw_k_gain(key, part):
    key = jax.random.fold_in(key, 17)
    return jax.random.uniform(key, (HEAD_DIM,), jnp.float32, 0.5, 2.0)


def draw_neighbours(key, part):
    key = jax.random.fold_in(key, 23)
    tile_rows = ROWS // TILE
    shifted = jax.random.randint(key, (TILES,), -1, 2, jnp.int32)
    numbers = jnp.arange(TILES, dtype=jnp.int32)
    tile_row = numbers // TILE_COLS
    center = numbers % TILE_COLS + shifted
    row_steps = jnp.array([-1, -1, -1, 0, 0, 0, 1, 1, 1], jnp.int32)
    col_steps = jnp.array([-1, 0, 1, -1, 0, 1, -1, 0, 1], jnp.int32)
    near_rows = tile_row[:, None] + row_steps[None, :]
    near_cols = center[:, None] + col_steps[None, :]
    inside = (near_rows >= 0) & (near_rows < tile_rows) & (near_cols >= 0) & (near_cols < TILE_COLS)
    listed = jnp.where(inside, near_rows * TILE_COLS + near_cols, -1)
    ordering = (1 - inside.astype(jnp.int32)) * 9 + jnp.arange(9, dtype=jnp.int32)[None, :]
    placed = jnp.argsort(ordering, axis=1)
    return jnp.take_along_axis(listed, placed, axis=1).astype(jnp.int32)


def draw_tile_owner(key, part):
    key = jax.random.fold_in(key, 37)
    device_key, column_key = jax.random.split(key)
    tile_rows = ROWS // TILE
    device_order = jax.random.permutation(device_key, ROWS)
    row_keys = jax.random.split(column_key, tile_rows)
    column_order = jax.vmap(lambda row_key: jax.random.permutation(row_key, TILE_COLS))(row_keys)
    position = (jnp.arange(tile_rows, dtype=jnp.int32)[:, None] * TILE_COLS + column_order) % ROWS
    return device_order[position].reshape(-1).astype(jnp.int32)


def block_levels(stream_key, extent, cuts, low, top_value):
    level = 1.0
    for axis_at, parts in cuts:
        heights = jax.random.uniform(jax.random.fold_in(jax.random.fold_in(stream_key, 6), axis_at), (parts,), jnp.float32, low / len(cuts), top_value / len(cuts))
        level = level * jnp.repeat(jnp.exp(heights), extent[axis_at] // parts).reshape((-1,) + (1,) * (len(extent) - 1 - axis_at))
    return level


def noise(key, shape, width, most, shards=(), held_as=jnp.bfloat16):
    level = block_levels(key, shape, shards, -0.22, 0.18) if shards else 1.0
    values = jax.random.normal(key, shape, jnp.float32) * width * level
    return jnp.minimum(jnp.maximum(values, -most), most).astype(held_as)


def setup_inputs(seed: int = 0) -> dict:
    streams_of = jax.random.split(jax.random.key(seed), 8)
    return {
        "latent": noise(streams_of[0], (FRAMES, ROWS, COLS, D), 1.0, 6.0, ((1, 32), (2, 8))),
        "w_qkv": draw_w_qkv(jax.random.fold_in(streams_of[7], 71), 0),
        "q_gain": draw_q_gain(jax.random.fold_in(streams_of[7], 71), 0),
        "k_gain": draw_k_gain(jax.random.fold_in(streams_of[7], 71), 0),
        "w_out": noise(streams_of[4], (HEADS * HEAD_DIM, D), (HEADS * HEAD_DIM) ** -0.5, 0.109375, ((0, 8),)),
        "neighbours": draw_neighbours(jax.random.fold_in(streams_of[7], 71), 0),
        "tile_owner": draw_tile_owner(jax.random.fold_in(streams_of[7], 71), 0),
    }


epsilon = 1e-06

def head_norm(values, gain):
    scaled = values * lax.rsqrt(lax.optimization_barrier(jnp.mean(values * values, axis=-1, keepdims=True)) + epsilon)
    return scaled * gain

def to_tiles(field):
    tile_rows = ROWS // TILE
    shaped = field.reshape(FRAMES, tile_rows, TILE, TILE_COLS, TILE, HEADS, HEAD_DIM)
    shaped = jnp.transpose(shaped, (1, 3, 0, 2, 4, 5, 6))
    return shaped.reshape(TILES, TILE_TOKENS, HEADS, HEAD_DIM)

def reference(latent, w_qkv, q_gain, k_gain, w_out, neighbours, tile_owner):
    token_rows = latent.reshape(-1, D)
    projected = jnp.dot(token_rows, w_qkv.reshape(D, 3 * HEADS * HEAD_DIM), preferred_element_type=jnp.float32)
    projected = projected.reshape(FRAMES, ROWS, COLS, 3, HEADS, HEAD_DIM)
    queries = to_tiles(head_norm(projected[:, :, :, 0], q_gain).astype(jnp.bfloat16))
    key_rows = to_tiles(head_norm(projected[:, :, :, 1], k_gain).astype(jnp.bfloat16))
    value_rows = to_tiles(projected[:, :, :, 2].astype(jnp.bfloat16))
    score_scale = HEAD_DIM ** (-0.5)

    def attend_tile(operands):
        query_tile, window = operands
        picked = jnp.maximum(window, 0).astype(jnp.int32)
        window_keys = key_rows[picked].reshape(-1, HEADS, HEAD_DIM).astype(jnp.float32)
        window_values = value_rows[picked].reshape(-1, HEADS, HEAD_DIM).astype(jnp.float32)
        allowed = jnp.repeat(window >= 0, TILE_TOKENS)
        scores = jnp.einsum('qhd,khd->hqk', query_tile.astype(jnp.float32), window_keys) * score_scale
        scores = jnp.where(allowed[None, None, :], scores, -jnp.inf)
        row_max = lax.optimization_barrier(jnp.max(scores, axis=-1, keepdims=True))
        weights = jnp.exp(scores - row_max)
        probabilities = (weights / lax.optimization_barrier(jnp.sum(weights, axis=-1, keepdims=True))).astype(jnp.bfloat16)
        attended_tile = jnp.einsum('hqk,khd->qhd', probabilities.astype(jnp.float32), window_values)
        return attended_tile.astype(jnp.bfloat16)
    attended = lax.map(attend_tile, (queries, neighbours))
    attended = attended.reshape(TILES * TILE_TOKENS, HEADS * HEAD_DIM)
    group_width = HEADS * HEAD_DIM // N_HEAD
    total = jnp.zeros((TILES * TILE_TOKENS, D), jnp.float32)
    for group in range(N_HEAD):
        term = jnp.dot(attended[:, group * group_width:(group + 1) * group_width], w_out[group * group_width:(group + 1) * group_width], preferred_element_type=jnp.float32)
        rounded = lax.optimization_barrier(term.astype(jnp.bfloat16))
        total = total + rounded.astype(jnp.float32)
    mixed = total.astype(jnp.bfloat16).reshape(TILES, TILE_TOKENS, D)
    numbers = jnp.arange(TILES, dtype=jnp.int32)
    same_owner = tile_owner[None, :] == tile_owner[:, None]
    earlier = numbers[None, :] < numbers[:, None]
    rank_within = lax.optimization_barrier(jnp.sum((same_owner & earlier).astype(jnp.int32), axis=1)).astype(jnp.int32)
    target_slot = (tile_owner * TILES_DEV + rank_within).astype(jnp.int32)
    return jnp.zeros_like(mixed).at[target_slot].set(mixed)
```

```python
import functools

import jax
import jax.numpy as jnp
from jax import lax
from jax.experimental import pallas as pl
from jax.experimental.pallas import tpu as pltpu
from jax.sharding import PartitionSpec as P

D = 3072
HEAD_DIM = 128
FRAMES = 4
TILE = 8
TILE_COLS = 8
TILES = 32
TILE_TOKENS = 256
N_HEAD = 8
PLANE = 4
PLANES = 8
PIECE = FRAMES * TILE
WIDTH = 384
HEADS_HERE = 3
SLOTS = 6
WINDOW = 3 * PIECE
KEYS = SLOTS * WINDOW
SCORE_SCALE = HEAD_DIM ** (-0.5) * 1.4426950408889634

epsilon = 1e-06
VMEM_LIMIT = 40 * 1024 * 1024


def params():
    return pltpu.CompilerParams(vmem_limit_bytes=VMEM_LIMIT)


def project_kernel(place, *refs):
    pieces, (w_ref, gain_ref, q_ref, kv_ref, rows) = refs[:N_HEAD], refs[N_HEAD:]
    step = pl.program_id(0)

    @pl.when(step == 0)
    def _():
        for k in range(N_HEAD):
            start = pl.multiple_of(place[k] * PIECE, PIECE)
            rows[pl.ds(start, PIECE), :] = pieces[k][...]

    result = jnp.dot(rows[...], w_ref[...], preferred_element_type=jnp.float32)

    def normed(gain):
        heads = []
        for h in range(HEADS_HERE):
            part = result[:, h * HEAD_DIM : (h + 1) * HEAD_DIM]
            mean = jnp.mean(part * part, axis=-1, keepdims=True)
            heads.append((part * lax.rsqrt(mean + epsilon) * gain).astype(jnp.bfloat16))
        return jnp.concatenate(heads, axis=1)

    @pl.when(step == 0)
    def _():
        q_ref[...] = normed(gain_ref[0:1, :])

    @pl.when(step == 1)
    def _():
        kv_ref[...] = normed(gain_ref[1:2, :])

    @pl.when(step == 2)
    def _():
        kv_ref[...] = result.astype(jnp.bfloat16)


def project(place, pieces, weight, gains):
    tokens = N_HEAD * PIECE
    grid_spec = pltpu.PrefetchScalarGridSpec(
        num_scalar_prefetch=1,
        grid=(3,),
        in_specs=[pl.BlockSpec((PIECE, D), lambda p, s: (0, 0))] * N_HEAD
        + [
            pl.BlockSpec((D, WIDTH), lambda p, s: (0, p)),
            pl.BlockSpec((2, HEAD_DIM), lambda p, s: (0, 0)),
        ],
        out_specs=[
            pl.BlockSpec((tokens, WIDTH), lambda p, s: (0, 0)),
            pl.BlockSpec((tokens, WIDTH), lambda p, s: (0, jnp.maximum(p - 1, 0))),
        ],
        scratch_shapes=[pltpu.VMEM((tokens, D), jnp.bfloat16)],
    )
    return pl.pallas_call(
        project_kernel,
        grid_spec=grid_spec,
        out_shape=[
            jax.ShapeDtypeStruct((tokens, WIDTH), jnp.bfloat16),
            jax.ShapeDtypeStruct((tokens, 2 * WIDTH), jnp.bfloat16),
        ],
        compiler_params=params(),
        cost_estimate=pl.CostEstimate(
            flops=2 * tokens * D * 3 * WIDTH, bytes_accessed=10_000_000, transcendentals=0
        ),
        name="project",
    )(place, *pieces, weight, gains)


def attend_kernel(starts, *refs):
    queries, slots = refs[:PLANE], refs[PLANE : PLANE + SLOTS]
    bias_ref = refs[PLANE + SLOTS]
    outs = refs[PLANE + SLOTS + 1 : 2 * PLANE + SLOTS + 1]
    level_ref = refs[2 * PLANE + SLOTS + 1]
    lanes = lax.broadcasted_iota(jnp.int32, (PLANE * PIECE, HEAD_DIM), 1)
    level_ref[...] = jnp.zeros_like(level_ref)

    def column(c, carry):
        here = pl.ds(pl.multiple_of(c * PIECE, PIECE), PIECE)
        window = pl.ds(pl.multiple_of(starts[c] * PIECE, PIECE), WINDOW)
        bias = bias_ref[c]
        levels = level_ref[...]
        for h in range(HEADS_HERE):
            head = slice(h * HEAD_DIM, (h + 1) * HEAD_DIM)
            value_head = slice(WIDTH + h * HEAD_DIM, WIDTH + (h + 1) * HEAD_DIM)
            q = jnp.concatenate([ref[here, head] for ref in queries], axis=0)
            keys = jnp.concatenate([ref[window, head] for ref in slots], axis=0)
            values = jnp.concatenate([ref[window, value_head] for ref in slots], axis=0)
            scores = lax.dot_general(
                q, keys, (((1,), (1,)), ((), ())), preferred_element_type=jnp.float32
            )
            scores = scores * SCORE_SCALE + bias
            top = jnp.max(scores, axis=-1, keepdims=True)
            weights = jnp.exp2(scores - top)
            total = jnp.sum(weights, axis=-1, keepdims=True)
            mixed = jnp.dot(
                weights.astype(jnp.bfloat16), values, preferred_element_type=jnp.float32
            )
            mixed = (mixed / total).astype(jnp.bfloat16)
            for k in range(PLANE):
                outs[k][here, head] = mixed[k * PIECE : (k + 1) * PIECE]
            levels = jnp.where(lanes == HEADS_HERE * c + h, top + jnp.log2(total), levels)
        level_ref[...] = levels
        return carry

    lax.fori_loop(0, TILE_COLS, column, 0)


def attend(starts, queries, slots, bias):
    tokens = TILE_COLS * PIECE
    whole = pl.BlockSpec(memory_space=pltpu.VMEM)
    return pl.pallas_call(
        attend_kernel,
        in_specs=[pl.BlockSpec(memory_space=pltpu.SMEM)] + [whole] * (PLANE + SLOTS + 1),
        out_specs=[whole] * (PLANE + 1),
        out_shape=[jax.ShapeDtypeStruct((tokens, WIDTH), jnp.bfloat16)] * PLANE
        + [jax.ShapeDtypeStruct((PLANE * PIECE, HEAD_DIM), jnp.float32)],
        compiler_params=params(),
        cost_estimate=pl.CostEstimate(
            flops=4 * PLANE * tokens * KEYS * WIDTH, bytes_accessed=5_000_000, transcendentals=2_000_000
        ),
        name="attend",
    )(starts, *queries, *slots, bias)


def join_kernel(place, *refs):
    shares, levels = refs[:PLANE], refs[PLANE : 2 * PLANE]
    w_ref = refs[2 * PLANE]
    outs = refs[2 * PLANE + 1 : 2 * PLANE + 1 + N_HEAD]
    joined = refs[-1]
    level = [ref[...] for ref in levels]
    top = functools.reduce(jnp.maximum, level)
    weight = [jnp.exp2(value - top) for value in level]
    scale = 1.0 / functools.reduce(jnp.add, weight)
    weight = [value * scale for value in weight]
    for c in range(TILE_COLS):
        rows = slice(c * PIECE, (c + 1) * PIECE)
        for h in range(HEADS_HERE):
            head = slice(h * HEAD_DIM, (h + 1) * HEAD_DIM)
            lane = HEADS_HERE * c + h
            total = None
            for k in range(PLANE):
                term = weight[k][:, lane : lane + 1] * shares[k][rows, head].astype(jnp.float32)
                total = term if total is None else total + term
            joined[rows, head] = total.astype(jnp.bfloat16)
    attended = joined[...]
    for k in range(N_HEAD):
        columns = pl.ds(pl.multiple_of(place[k] * WIDTH, WIDTH), WIDTH)
        outs[k][...] = jnp.dot(
            attended, w_ref[:, columns], preferred_element_type=jnp.float32
        ).astype(jnp.bfloat16)


def join(place, shares, levels, w_out):
    tokens = TILE_COLS * PIECE
    whole = pl.BlockSpec(memory_space=pltpu.VMEM)
    return pl.pallas_call(
        join_kernel,
        in_specs=[pl.BlockSpec(memory_space=pltpu.SMEM)] + [whole] * (2 * PLANE + 1),
        out_specs=[whole] * N_HEAD,
        out_shape=[jax.ShapeDtypeStruct((tokens, WIDTH), jnp.bfloat16)] * N_HEAD,
        scratch_shapes=[pltpu.VMEM((tokens, WIDTH), jnp.bfloat16)],
        compiler_params=params(),
        cost_estimate=pl.CostEstimate(
            flops=2 * tokens * WIDTH * D, bytes_accessed=5_000_000, transcendentals=0
        ),
        name="join",
    )(place, *shares, *levels, w_out)


def total_kernel(picks, *refs):
    terms, (out_ref, rows) = refs[:N_HEAD], refs[N_HEAD:]
    total = terms[0][...].astype(jnp.float32)
    for ref in terms[1:]:
        total = total + ref[...].astype(jnp.float32)
    rows[...] = total.astype(jnp.bfloat16)

    def copy(d, carry):
        start = pl.multiple_of(picks[d] * PIECE, PIECE)
        to = pl.multiple_of(d * PIECE, PIECE)
        out_ref[pl.ds(to, PIECE), :] = rows[pl.ds(start, PIECE), :]
        return carry

    lax.fori_loop(0, TILES, copy, 0)


def add_terms(picks, terms):
    tokens = TILE_COLS * PIECE
    whole = pl.BlockSpec(memory_space=pltpu.VMEM)
    return pl.pallas_call(
        total_kernel,
        in_specs=[pl.BlockSpec(memory_space=pltpu.SMEM)] + [whole] * N_HEAD,
        out_specs=whole,
        out_shape=jax.ShapeDtypeStruct((TILES * PIECE, WIDTH), jnp.bfloat16),
        scratch_shapes=[pltpu.VMEM((tokens, WIDTH), jnp.bfloat16)],
        compiler_params=params(),
        cost_estimate=pl.CostEstimate(flops=800_000, bytes_accessed=3_000_000, transcendentals=0),
        name="add_terms",
    )(picks, *terms)


def tile_kernel(row, arrived, out_ref):
    base = row[0] * (TILE * PIECE)
    pieces = [
        arrived[pl.ds(pl.multiple_of(base + j * PIECE, PIECE), PIECE), :].astype(jnp.float32)
        for j in range(TILE)
    ]
    parts = [
        pieces[j][f * TILE : (f + 1) * TILE] for f in range(FRAMES) for j in range(TILE)
    ]
    out_ref[...] = jnp.concatenate(parts, axis=0).astype(jnp.bfloat16)


def to_tile(row, arrived):
    whole = pl.BlockSpec(memory_space=pltpu.VMEM)
    return pl.pallas_call(
        tile_kernel,
        in_specs=[pl.BlockSpec(memory_space=pltpu.SMEM), whole],
        out_specs=whole,
        out_shape=jax.ShapeDtypeStruct((TILE_TOKENS, WIDTH), jnp.bfloat16),
        compiler_params=params(),
        cost_estimate=pl.CostEstimate(flops=100_000, bytes_accessed=1_000_000, transcendentals=0),
        name="to_tile",
    )(row, arrived)


def head_swap(array, k):
    return lax.ppermute(array, "head", [(h, h ^ k) for h in range(N_HEAD)])


def plane_swap(array, k):
    return lax.ppermute(array, "seq", [(s, s ^ k) for s in range(PLANE * PLANES)])


def shift(array, d):
    pairs = [
        (z * PLANE + i, (z + d) * PLANE + i)
        for z in range(PLANES)
        if 0 <= z + d < PLANES
        for i in range(PLANE)
    ]
    return lax.ppermute(array, "seq", pairs)


def local(latent, w_qkv, q_gain, k_gain, w_out, neighbours, tile_owner):
    position = lax.axis_index("seq")
    group = lax.axis_index("head")
    plane = position // PLANE
    odd = plane % 2
    tile_row = position // TILE
    place = jnp.bitwise_xor(group, jnp.arange(N_HEAD, dtype=jnp.int32))

    piece = latent.reshape(PIECE, D)
    pieces = [piece] + [head_swap(piece, k) for k in range(1, N_HEAD)]
    gains = jnp.stack([q_gain, k_gain])
    queries, keys = project(place, pieces, w_qkv.reshape(D, 3 * WIDTH), gains)

    all_queries = [queries] + [plane_swap(queries, k) for k in range(1, PLANE)]
    below_1, above_1 = shift(keys, 1), shift(keys, -1)
    below_2, above_2 = shift(below_1, 1), shift(above_1, -1)
    far = plane_swap(jnp.where(odd == 1, above_2, below_2), PLANE)
    slots = [keys, below_1, above_1, below_2, above_2, far]

    lists = lax.dynamic_slice_in_dim(neighbours, tile_row * TILE_COLS, TILE_COLS, 0)
    columns = jnp.where(lists >= 0, lists % TILE_COLS, TILE_COLS)
    starts = jnp.minimum(jnp.min(columns, axis=1), TILE_COLS - 3)
    slot_plane = plane + jnp.stack(
        [jnp.int32(0), jnp.int32(-1), jnp.int32(1), jnp.int32(-2), jnp.int32(2), 3 - 6 * odd]
    )
    inside = (slot_plane >= 0) & (slot_plane < PLANES)
    key_tile = (slot_plane // 2)[None, :, None] * TILE_COLS + (
        starts[:, None, None] + jnp.arange(3, dtype=jnp.int32)[None, None, :]
    )
    allowed = jnp.any(key_tile[..., None] == lists[:, None, None, :], axis=-1) & inside[None, :, None]
    bias = jnp.where(allowed, 0.0, -jnp.inf).astype(jnp.float32)
    bias = jnp.broadcast_to(bias[..., None], (TILE_COLS, SLOTS, 3, PIECE)).reshape(TILE_COLS, 1, KEYS)

    *shares, level = attend(starts, all_queries, slots, bias)
    levels = [level[k * PIECE : (k + 1) * PIECE] for k in range(PLANE)]
    shares = [shares[0]] + [plane_swap(shares[k], k) for k in range(1, PLANE)]
    levels = [levels[0]] + [plane_swap(levels[k], k) for k in range(1, PLANE)]

    terms = join(place, shares, levels, w_out)
    terms = [terms[0]] + [head_swap(terms[k], k) for k in range(1, N_HEAD)]

    numbers = jnp.arange(TILES, dtype=jnp.int32)
    owned = tile_owner[None, :] == numbers[:, None]
    tile_of = jnp.sum(jnp.where(owned, numbers[None, :], 0), axis=1)
    sent = add_terms(tile_of % TILE_COLS, terms)
    arrived = lax.all_to_all(
        sent.reshape(TILES, PIECE, WIDTH), "seq", split_axis=0, concat_axis=0, tiled=True
    )
    own_row = (tile_of[position] // TILE_COLS).reshape(1)
    return to_tile(own_row, arrived.reshape(TILES * PIECE, WIDTH)).reshape(1, TILE_TOKENS, WIDTH)


def solution(mesh):
    placed = (
        P(None, "seq", "head", None),
        P(None, None, "head"),
        P(),
        P(),
        P("head", None),
        P(),
        P(),
    )
    return jax.shard_map(
        local, mesh=mesh, in_specs=placed, out_specs=P("seq", None, "head"), check_vma=False
    )
```

```python
import functools

import jax
import jax.numpy as jnp
from jax import lax
from jax.experimental import pallas as pl
from jax.experimental.pallas import tpu as pltpu
from jax.sharding import PartitionSpec as P

D = 3072
HEAD_DIM = 128
FRAMES = 4
TILE = 8
TILE_COLS = 8
TILES = 32
TILE_TOKENS = 256
N_HEAD = 8
PLANE = 4
PLANES = 8
PIECE = FRAMES * TILE
PAIR = 2 * TILE
WIDTH = 384
HEADS_HERE = 3
SLOTS = 6
WINDOW = 3 * PIECE
SCORE_SCALE = HEAD_DIM ** (-0.5) * 1.4426950408889634

LOADS = 4

epsilon = 1e-06
LOWEST = -1e30


def params(mib):
    return pltpu.CompilerParams(vmem_limit_bytes=mib * 1024 * 1024)


def plan_kernel(ids, neighbours, tile_owner, starts, flags, tile_of, first, half):
    position = ids[0]
    tile_row = position // TILE
    odd = (position // PLANE) % 2
    for c in range(TILE_COLS):
        tile = tile_row * TILE_COLS + c
        start = jnp.int32(TILE_COLS - 3)
        for n in range(9):
            listed = neighbours[tile, n]
            start = jnp.where(listed >= 0, jnp.minimum(start, listed % TILE_COLS), start)
        starts[c] = start
        for n in range(9):
            flags[c, n] = 0
        for n in range(9):
            listed = neighbours[tile, n]

            @pl.when(listed >= 0)
            def _():
                step = listed // TILE_COLS - tile_row
                kind = jnp.where(step == 0, 0, jnp.where((step > 0) == (odd == 1), 1, 2))
                flags[c, kind * 3 + listed % TILE_COLS - start] = 1

    for t in range(TILES):
        tile_of[tile_owner[t]] = t
    first[0] = tile_of[position] // (2 * TILE_COLS)
    half[0] = tile_row % 2


def plan(ids, neighbours, tile_owner):
    scalars = pl.BlockSpec(memory_space=pltpu.SMEM)
    shapes = [(TILE_COLS,), (TILE_COLS, 9), (TILES,), (1,), (1,)]
    return pl.pallas_call(
        plan_kernel,
        in_specs=[scalars] * 3,
        out_specs=[scalars] * len(shapes),
        out_shape=[jax.ShapeDtypeStruct(shape, jnp.int32) for shape in shapes],
        compiler_params=params(8),
        cost_estimate=pl.CostEstimate(flops=0, bytes_accessed=8_000_000, transcendentals=0),
        name="plan",
    )(ids, neighbours, tile_owner)


def normed(result, gain):
    heads = []
    for h in range(HEADS_HERE):
        part = result[:, h * HEAD_DIM : (h + 1) * HEAD_DIM]
        mean = jnp.mean(part * part, axis=-1, keepdims=True)
        heads.append((part * lax.rsqrt(mean + epsilon) * gain).astype(jnp.bfloat16))
    return jnp.concatenate(heads, axis=1)


def gather_rows(ids, pieces, rows):
    for k, piece in enumerate(pieces):
        start = pl.multiple_of((ids[1] ^ k) * PIECE, PIECE)
        rows[pl.ds(start, PIECE), :] = piece[...]


def load_kernel(w_ref, out_ref, sems):
    rows = D // LOADS
    copies = []
    for n in range(3):
        for e in range(LOADS):
            part = pl.ds(e * rows, rows)
            copies.append(
                pltpu.make_async_copy(w_ref.at[n, part], out_ref.at[n, part], sems.at[n, e])
            )
    for copy in copies:
        copy.start()
    for copy in copies:
        copy.wait()


def load_weight(weight):
    return pl.pallas_call(
        load_kernel,
        in_specs=[pl.BlockSpec(memory_space=pltpu.HBM)],
        out_specs=pl.BlockSpec(memory_space=pltpu.VMEM),
        out_shape=jax.ShapeDtypeStruct(weight.shape, weight.dtype),
        scratch_shapes=[pltpu.SemaphoreType.DMA((3, LOADS))],
        compiler_params=params(8),
        cost_estimate=pl.CostEstimate(flops=0, bytes_accessed=7_100_000, transcendentals=0),
        name="load_weight",
    )(weight)


def queries_kernel(ids, *refs):
    pieces, (w_ref, gain_ref, out_ref, rows_ref) = refs[:N_HEAD], refs[N_HEAD:]
    gather_rows(ids, pieces, rows_ref)
    result = jnp.dot(rows_ref[...], w_ref[0], preferred_element_type=jnp.float32)
    out_ref[...] = normed(result, gain_ref[...])


def project_queries(ids, pieces, weight, gain):
    tokens = N_HEAD * PIECE
    whole = pl.BlockSpec(memory_space=pltpu.VMEM)
    return pl.pallas_call(
        queries_kernel,
        in_specs=[pl.BlockSpec(memory_space=pltpu.SMEM)] + [whole] * (N_HEAD + 2),
        out_specs=[whole] * 2,
        out_shape=[
            jax.ShapeDtypeStruct((tokens, WIDTH), jnp.bfloat16),
            jax.ShapeDtypeStruct((tokens, D), jnp.bfloat16),
        ],
        compiler_params=params(16),
        cost_estimate=pl.CostEstimate(
            flops=2 * tokens * D * WIDTH, bytes_accessed=4_000_000, transcendentals=0
        ),
        name="project_queries",
    )(ids, *pieces, weight, gain)


def keys_kernel(rows_ref, w_ref, gain_ref, out_ref):
    rows = rows_ref[...]
    keys = jnp.dot(rows, w_ref[1], preferred_element_type=jnp.float32)
    out_ref[:, :WIDTH] = normed(keys, gain_ref[...])
    values = jnp.dot(rows, w_ref[2], preferred_element_type=jnp.float32)
    out_ref[:, WIDTH:] = values.astype(jnp.bfloat16)


def project_keys(rows, weight, gain):
    tokens = N_HEAD * PIECE
    whole = pl.BlockSpec(memory_space=pltpu.VMEM)
    return pl.pallas_call(
        keys_kernel,
        in_specs=[whole] * 3,
        out_specs=whole,
        out_shape=jax.ShapeDtypeStruct((tokens, 2 * WIDTH), jnp.bfloat16),
        compiler_params=params(16),
        cost_estimate=pl.CostEstimate(
            flops=2 * tokens * D * 2 * WIDTH, bytes_accessed=6_000_000, transcendentals=0
        ),
        name="project_keys",
    )(rows, weight, gain)


def attend_kernel(kinds, last, starts, flags, *refs):
    count = len(kinds)
    refs = list(refs)
    take = lambda n: [refs.pop(0) for _ in range(n)]
    queries, slots = take(PLANE), take(count)
    before = take(PLANE + 1) if last else None
    outs = take(PLANE) if last else take(PLANE + 1)
    piece_of = lax.broadcasted_iota(jnp.int32, (1, count * WINDOW), 1) // PIECE
    ones = jnp.ones((count * WINDOW, HEAD_DIM), jnp.bfloat16)
    level_ref = refs.pop(0) if last else outs[PLANE]
    level_ref[...] = jnp.zeros_like(level_ref)
    for c in range(TILE_COLS):
        here = slice(c * PIECE, (c + 1) * PIECE)
        window = pl.ds(pl.multiple_of(starts[c] * PIECE, PIECE), WINDOW)
        bias = jnp.full((1, count * WINDOW), -jnp.inf, jnp.float32)
        for n in range(3 * count):
            bias = jnp.where((piece_of == n) & (flags[c, kinds[n // 3] * 3 + n % 3] > 0), 0.0, bias)
        for h in range(HEADS_HERE):
            head = slice(h * HEAD_DIM, (h + 1) * HEAD_DIM)
            value_head = slice(WIDTH + h * HEAD_DIM, WIDTH + (h + 1) * HEAD_DIM)
            lane = slice(HEADS_HERE * c + h, HEADS_HERE * c + h + 1)
            q = jnp.concatenate([ref[here, head] for ref in queries], axis=0)
            k = jnp.concatenate([slot[window, head] for slot in slots], axis=0)
            v = jnp.concatenate([slot[window, value_head] for slot in slots], axis=0)
            scores = lax.dot_general(
                q, k, (((1,), (1,)), ((), ())), preferred_element_type=jnp.float32
            )
            scores = scores * SCORE_SCALE + bias
            top = jnp.maximum(jnp.max(scores, axis=-1, keepdims=True), LOWEST)
            weights = jnp.exp2(scores - top).astype(jnp.bfloat16)
            both = jnp.dot(
                weights, jnp.concatenate([v, ones], axis=1), preferred_element_type=jnp.float32
            )
            mixed, total = both[:, :HEAD_DIM], both[:, HEAD_DIM:]
            if last:
                other = before[PLANE][:, lane]
                mixed_before = jnp.concatenate([ref[here, head] for ref in before[:PLANE]], axis=0)
                high = jnp.maximum(top, other)
                share = jnp.exp2(other - high)
                mine = jnp.exp2(top - high)
                whole = mine * total + share
                mixed = (mixed * mine + mixed_before.astype(jnp.float32) * share) / whole
                level = high + jnp.log2(whole)
            else:
                mixed = mixed / total
                level = top + jnp.log2(total)
            mixed = mixed.astype(jnp.bfloat16)
            for n in range(PLANE):
                outs[n][here, head] = mixed[n * PIECE : (n + 1) * PIECE]
            level_ref[:, lane] = level[:, lane]
    if last:
        tail = slice(TILE_COLS * PIECE, (TILE_COLS + 1) * PIECE)
        rest = level_ref[...]
        for part in range(3):
            rounded = rest.astype(jnp.bfloat16)
            rest = rest - rounded.astype(jnp.float32)
            for n in range(PLANE):
                outs[n][tail, part * HEAD_DIM : (part + 1) * HEAD_DIM] = rounded[
                    n * PIECE : (n + 1) * PIECE
                ]


def attend(starts, flags, queries, slots, before=()):
    tokens = TILE_COLS * PIECE
    count = len(slots)
    last = bool(before)
    kinds = (1, 2, 2) if last else (0, 0, 1)
    whole = pl.BlockSpec(memory_space=pltpu.VMEM)
    scalars = pl.BlockSpec(memory_space=pltpu.SMEM)
    operands = [*queries, *slots, *before]
    levels = (PLANE * PIECE, HEAD_DIM)
    if last:
        out_shape = [jax.ShapeDtypeStruct((tokens + PIECE, WIDTH), jnp.bfloat16)] * PLANE
    else:
        out_shape = [jax.ShapeDtypeStruct((tokens, WIDTH), jnp.bfloat16)] * PLANE
        out_shape.append(jax.ShapeDtypeStruct(levels, jnp.float32))
    scratch = [pltpu.VMEM(levels, jnp.float32)] if last else []
    return pl.pallas_call(
        functools.partial(attend_kernel, kinds, last),
        in_specs=[scalars] * 2 + [whole] * len(operands),
        out_specs=[whole] * len(out_shape),
        out_shape=out_shape,
        scratch_shapes=scratch,
        compiler_params=params(16),
        cost_estimate=pl.CostEstimate(
            flops=4 * PLANE * tokens * count * WINDOW * WIDTH,
            bytes_accessed=4_000_000,
            transcendentals=1_000_000,
        ),
        name="attend",
    )(starts, flags, *operands)


def join_kernel(ids, *refs):
    shares, w_ref = refs[:PLANE], refs[PLANE]
    outs, joined = refs[PLANE + 1 : PLANE + 1 + N_HEAD], refs[-1]
    tail = slice(TILE_COLS * PIECE, (TILE_COLS + 1) * PIECE)
    level = []
    for ref in shares:
        parts = [
            ref[tail, n * HEAD_DIM : (n + 1) * HEAD_DIM].astype(jnp.float32) for n in range(3)
        ]
        level.append(parts[0] + (parts[1] + parts[2]))
    top = functools.reduce(jnp.maximum, level)
    weight = [jnp.exp2(value - top) for value in level]
    scale = 1.0 / functools.reduce(jnp.add, weight)
    weight = [value * scale for value in weight]
    for c in range(TILE_COLS):
        rows = slice(c * PIECE, (c + 1) * PIECE)
        for h in range(HEADS_HERE):
            head = slice(h * HEAD_DIM, (h + 1) * HEAD_DIM)
            lane = HEADS_HERE * c + h
            total = None
            for k in range(PLANE):
                term = weight[k][:, lane : lane + 1] * shares[k][rows, head].astype(jnp.float32)
                total = term if total is None else total + term
            joined[rows, head] = total.astype(jnp.bfloat16)
    attended = joined[...]
    for k in range(N_HEAD):
        columns = pl.ds(pl.multiple_of((ids[1] ^ k) * WIDTH, WIDTH), WIDTH)
        outs[k][...] = jnp.dot(
            attended, w_ref[:, columns], preferred_element_type=jnp.float32
        ).astype(jnp.bfloat16)


def join(ids, shares, w_out):
    tokens = TILE_COLS * PIECE
    whole = pl.BlockSpec(memory_space=pltpu.VMEM)
    return pl.pallas_call(
        join_kernel,
        in_specs=[pl.BlockSpec(memory_space=pltpu.SMEM)] + [whole] * (PLANE + 1),
        out_specs=[whole] * N_HEAD,
        out_shape=[jax.ShapeDtypeStruct((tokens, WIDTH), jnp.bfloat16)] * N_HEAD,
        scratch_shapes=[pltpu.VMEM((tokens, WIDTH), jnp.bfloat16)],
        compiler_params=params(16),
        cost_estimate=pl.CostEstimate(
            flops=2 * tokens * WIDTH * D, bytes_accessed=5_000_000, transcendentals=0
        ),
        name="join",
    )(ids, *shares, w_out)


def add_kernel(side, *refs):
    terms, (kept_ref, given_ref, rows) = refs[:N_HEAD], refs[N_HEAD:]
    total = terms[0][...].astype(jnp.float32)
    for ref in terms[1:]:
        total = total + ref[...].astype(jnp.float32)
    rows[...] = total.astype(jnp.bfloat16)
    for c in range(TILE_COLS):
        to = slice(c * PAIR, (c + 1) * PAIR)
        for ref, which in ((kept_ref, side[0]), (given_ref, 1 - side[0])):
            start = pl.multiple_of(c * PIECE + which * PAIR, PAIR)
            ref[to, :] = rows[pl.ds(start, PAIR), :]


def add_terms(side, terms):
    whole = pl.BlockSpec(memory_space=pltpu.VMEM)
    return pl.pallas_call(
        add_kernel,
        in_specs=[pl.BlockSpec(memory_space=pltpu.SMEM)] + [whole] * N_HEAD,
        out_specs=[whole] * 2,
        out_shape=[jax.ShapeDtypeStruct((TILE_COLS * PAIR, WIDTH), jnp.bfloat16)] * 2,
        scratch_shapes=[pltpu.VMEM((TILE_COLS * PIECE, WIDTH), jnp.bfloat16)],
        compiler_params=params(8),
        cost_estimate=pl.CostEstimate(flops=800_000, bytes_accessed=2_000_000, transcendentals=0),
        name="add_terms",
    )(side, *terms)


def order_kernel(side, tile_of, kept_ref, got_ref, out_ref, rows):
    size = TILE_COLS * PAIR
    for ref, which in ((kept_ref, side[0]), (got_ref, 1 - side[0])):
        rows[pl.ds(pl.multiple_of(which * size, size), size), :] = ref[...]
    for d in range(TILES):
        start = pl.multiple_of((tile_of[d] % (2 * TILE_COLS)) * PAIR, PAIR)
        out_ref[d * PAIR : (d + 1) * PAIR, :] = rows[pl.ds(start, PAIR), :]


def order(side, tile_of, kept, got):
    whole = pl.BlockSpec(memory_space=pltpu.VMEM)
    scalars = pl.BlockSpec(memory_space=pltpu.SMEM)
    return pl.pallas_call(
        order_kernel,
        in_specs=[scalars, scalars, whole, whole],
        out_specs=whole,
        out_shape=jax.ShapeDtypeStruct((TILES * PAIR, WIDTH), jnp.bfloat16),
        scratch_shapes=[pltpu.VMEM((2 * TILE_COLS * PAIR, WIDTH), jnp.bfloat16)],
        compiler_params=params(8),
        cost_estimate=pl.CostEstimate(flops=100_000, bytes_accessed=800_000, transcendentals=0),
        name="order",
    )(side, tile_of, kept, got)


def tile_kernel(first, arrived, out_ref):
    base = first[0] * (2 * TILE * PAIR)
    pieces = [
        arrived[pl.ds(pl.multiple_of(base + n * PAIR, PAIR), PAIR), :].astype(jnp.float32)
        for n in range(2 * TILE)
    ]
    parts = [
        pieces[(f // 2) * TILE + j][(f % 2) * TILE : (f % 2 + 1) * TILE]
        for f in range(FRAMES)
        for j in range(TILE)
    ]
    out_ref[...] = jnp.concatenate(parts, axis=0).astype(jnp.bfloat16)


def to_tile(first, arrived):
    whole = pl.BlockSpec(memory_space=pltpu.VMEM)
    return pl.pallas_call(
        tile_kernel,
        in_specs=[pl.BlockSpec(memory_space=pltpu.SMEM), whole],
        out_specs=whole,
        out_shape=jax.ShapeDtypeStruct((TILE_TOKENS, WIDTH), jnp.bfloat16),
        compiler_params=params(8),
        cost_estimate=pl.CostEstimate(flops=100_000, bytes_accessed=800_000, transcendentals=0),
        name="to_tile",
    )(first, arrived)


def head_swap(array, k):
    return lax.ppermute(array, "head", [(h, h ^ k) for h in range(N_HEAD)])


def plane_swap(array, k):
    return lax.ppermute(array, "seq", [(s, s ^ k) for s in range(PLANE * PLANES)])


def mate_swap(array):
    return plane_swap(array, PLANE)


def edge_swap(array):
    pairs = []
    for z in range(1, PLANES - 1, 2):
        for i in range(PLANE):
            pairs += [(z * PLANE + i, (z + 1) * PLANE + i), ((z + 1) * PLANE + i, z * PLANE + i)]
    return lax.ppermute(array, "seq", pairs)


def local(latent, w_qkv, q_gain, k_gain, w_out, neighbours, tile_owner):
    ids = jnp.stack([lax.axis_index("seq"), lax.axis_index("head")]).astype(jnp.int32)
    weight = load_weight(jnp.transpose(w_qkv, (1, 0, 2)))
    q_gain, k_gain = q_gain.reshape(1, HEAD_DIM), k_gain.reshape(1, HEAD_DIM)
    starts, flags, tile_of, first, half = plan(ids, neighbours, tile_owner)

    pieces = [latent.reshape(PIECE, D)]
    pieces += [head_swap(pieces[0], k) for k in range(1, N_HEAD)]

    queries, rows = project_queries(ids, pieces, weight, q_gain)
    all_queries = [queries] + [plane_swap(queries, k) for k in range(1, PLANE)]
    own = project_keys(rows, weight, k_gain)
    mate, edge = mate_swap(own), edge_swap(own)
    mate, edge, *all_queries = lax.optimization_barrier((mate, edge, *all_queries))
    far_1, edge_2 = mate_swap(edge), edge_swap(mate)
    far_2 = mate_swap(edge_2)
    near = attend(starts, flags, all_queries, [own, mate, edge])
    shares = attend(starts, flags, all_queries, [edge_2, far_1, far_2], near)
    shares = [shares[0]] + [plane_swap(shares[k], k) for k in range(1, PLANE)]

    terms = join(ids, shares, w_out)
    terms = [terms[0]] + [head_swap(terms[k], k) for k in range(1, N_HEAD)]

    kept, given = add_terms(half, terms)
    sent = order(half, tile_of, kept, plane_swap(given, TILE))
    arrived = lax.all_to_all(
        sent.reshape(TILES, PAIR, WIDTH), "seq", split_axis=0, concat_axis=0, tiled=True
    )
    return to_tile(first, arrived.reshape(TILES * PAIR, WIDTH)).reshape(1, TILE_TOKENS, WIDTH)


def solution(mesh):
    placed = (
        P(None, "seq", "head", None),
        P(None, None, "head"),
        P(),
        P(),
        P("head", None),
        P(),
        P(),
    )
    return jax.shard_map(
        local, mesh=mesh, in_specs=placed, out_specs=P("seq", None, "head"), check_vma=False
    )
```

```python
import functools

import jax
import jax.numpy as jnp
from jax import lax
from jax.experimental import pallas as pl
from jax.experimental.pallas import tpu as pltpu
from jax.sharding import PartitionSpec as P

D = 3072
HEAD_DIM = 128
FRAMES = 4
TILE = 8
TILE_COLS = 8
TILES = 32
TILE_TOKENS = 256
N_HEAD = 8
PLANE = 4
PLANES = 8
PIECE = FRAMES * TILE
PAIR = 2 * TILE
WIDTH = 384
HEADS_HERE = 3
SLOTS = 6
WINDOW = 3 * PIECE
SCORE_SCALE = HEAD_DIM ** (-0.5) * 1.4426950408889634

LOADS = 4

RELAYED = (4, 5)
DIRECT = (0, 1, 2, 7, 6, 3)

epsilon = 1e-06
LOWEST = -1e30


def params(mib):
    return pltpu.CompilerParams(vmem_limit_bytes=mib * 1024 * 1024)


def plan_kernel(ids, neighbours, tile_owner, starts, flags, tile_of, first, half):
    position = ids[0]
    tile_row = position // TILE
    odd = (position // PLANE) % 2
    for c in range(TILE_COLS):
        tile = tile_row * TILE_COLS + c
        start = jnp.minimum(neighbours[0, tile] % TILE_COLS, TILE_COLS - 3)
        starts[c] = start
        for n in range(9):
            flags[c, n] = 0
        for n in range(9):
            listed = neighbours[n, tile]

            @pl.when(listed >= 0)
            def _():
                step = listed // TILE_COLS - tile_row
                kind = jnp.where(step == 0, 0, jnp.where((step > 0) == (odd == 1), 1, 2))
                flags[c, kind * 3 + listed % TILE_COLS - start] = 1

    for t in range(TILES):
        tile_of[tile_owner[t]] = t
    first[0] = tile_of[position] // (2 * TILE_COLS)
    half[0] = tile_row % 2


def plan(ids, neighbours, tile_owner):
    scalars = pl.BlockSpec(memory_space=pltpu.SMEM)
    shapes = [(TILE_COLS,), (TILE_COLS, 9), (TILES,), (1,), (1,)]
    return pl.pallas_call(
        plan_kernel,
        in_specs=[scalars] * 3,
        out_specs=[scalars] * len(shapes),
        out_shape=[jax.ShapeDtypeStruct(shape, jnp.int32) for shape in shapes],
        compiler_params=params(8),
        cost_estimate=pl.CostEstimate(flops=0, bytes_accessed=8_000_000, transcendentals=0),
        name="plan",
    )(ids, neighbours, tile_owner)


def normed(result, gain):
    heads = []
    for h in range(HEADS_HERE):
        part = result[:, h * HEAD_DIM : (h + 1) * HEAD_DIM]
        mean = jnp.mean(part * part, axis=-1, keepdims=True)
        heads.append((part * lax.rsqrt(mean + epsilon) * gain).astype(jnp.bfloat16))
    return jnp.concatenate(heads, axis=1)


def gather_rows(ids, pieces, rows):
    for k, piece in enumerate(pieces):
        start = pl.multiple_of((ids[1] ^ k) * PIECE, PIECE)
        rows[pl.ds(start, PIECE), :] = piece[...]


def load_kernel(w_ref, out_ref, sems):
    rows = D // LOADS
    copies = []
    for n in range(3):
        for e in range(LOADS):
            part = pl.ds(e * rows, rows)
            copies.append(
                pltpu.make_async_copy(w_ref.at[n, part], out_ref.at[n, part], sems.at[n, e])
            )
    for copy in copies:
        copy.start()
    for copy in copies:
        copy.wait()


def load_weight(weight):
    return pl.pallas_call(
        load_kernel,
        in_specs=[pl.BlockSpec(memory_space=pltpu.HBM)],
        out_specs=pl.BlockSpec(memory_space=pltpu.VMEM),
        out_shape=jax.ShapeDtypeStruct(weight.shape, weight.dtype),
        scratch_shapes=[pltpu.SemaphoreType.DMA((3, LOADS))],
        compiler_params=params(8),
        cost_estimate=pl.CostEstimate(flops=0, bytes_accessed=7_100_000, transcendentals=0),
        name="load_weight",
    )(weight)


def queries_kernel(ids, *refs):
    pieces, (w_ref, gain_ref, out_ref, rows_ref) = refs[:N_HEAD], refs[N_HEAD:]
    gather_rows(ids, pieces, rows_ref)
    result = jnp.dot(rows_ref[...], w_ref[0], preferred_element_type=jnp.float32)
    out_ref[...] = normed(result, gain_ref[...])


def project_queries(ids, pieces, weight, gain):
    tokens = N_HEAD * PIECE
    whole = pl.BlockSpec(memory_space=pltpu.VMEM)
    return pl.pallas_call(
        queries_kernel,
        in_specs=[pl.BlockSpec(memory_space=pltpu.SMEM)] + [whole] * (N_HEAD + 2),
        out_specs=[whole] * 2,
        out_shape=[
            jax.ShapeDtypeStruct((tokens, WIDTH), jnp.bfloat16),
            jax.ShapeDtypeStruct((tokens, D), jnp.bfloat16),
        ],
        compiler_params=params(16),
        cost_estimate=pl.CostEstimate(
            flops=2 * tokens * D * WIDTH, bytes_accessed=4_000_000, transcendentals=0
        ),
        name="project_queries",
    )(ids, *pieces, weight, gain)


def keys_kernel(rows_ref, w_ref, gain_ref, out_ref):
    rows = rows_ref[...]
    keys = jnp.dot(rows, w_ref[1], preferred_element_type=jnp.float32)
    out_ref[:, :WIDTH] = normed(keys, gain_ref[...])
    values = jnp.dot(rows, w_ref[2], preferred_element_type=jnp.float32)
    out_ref[:, WIDTH:] = values.astype(jnp.bfloat16)


def project_keys(rows, weight, gain):
    tokens = N_HEAD * PIECE
    whole = pl.BlockSpec(memory_space=pltpu.VMEM)
    return pl.pallas_call(
        keys_kernel,
        in_specs=[whole] * 3,
        out_specs=whole,
        out_shape=jax.ShapeDtypeStruct((tokens, 2 * WIDTH), jnp.bfloat16),
        compiler_params=params(16),
        cost_estimate=pl.CostEstimate(
            flops=2 * tokens * D * 2 * WIDTH, bytes_accessed=6_000_000, transcendentals=0
        ),
        name="project_keys",
    )(rows, weight, gain)


TAIL = slice(TILE_COLS * PIECE, (TILE_COLS + 1) * PIECE)


def store_level(ref, level):
    for n in range(3):
        rounded = level.astype(jnp.bfloat16)
        level = level - rounded.astype(jnp.float32)
        ref[TAIL, n * HEAD_DIM : (n + 1) * HEAD_DIM] = rounded


def load_level(ref):
    parts = [ref[TAIL, n * HEAD_DIM : (n + 1) * HEAD_DIM].astype(jnp.float32) for n in range(3)]
    return parts[0] + (parts[1] + parts[2])


def merge(shares, out_ref):
    levels = [load_level(ref) for ref in shares]
    top = functools.reduce(jnp.maximum, levels)
    weights = [jnp.exp2(level - top) for level in levels]
    total = functools.reduce(jnp.add, weights)
    weights = [weight / total for weight in weights]
    for c in range(TILE_COLS):
        rows = slice(c * PIECE, (c + 1) * PIECE)
        for h in range(HEADS_HERE):
            head = slice(h * HEAD_DIM, (h + 1) * HEAD_DIM)
            lane = HEADS_HERE * c + h
            mixed = None
            for weight, ref in zip(weights, shares):
                term = weight[:, lane : lane + 1] * ref[rows, head].astype(jnp.float32)
                mixed = term if mixed is None else mixed + term
            out_ref[rows, head] = mixed.astype(jnp.bfloat16)
    return top + jnp.log2(total)


def merge_kernel(first_ref, second_ref, out_ref):
    store_level(out_ref, merge([first_ref, second_ref], out_ref))


def merge_shares(first, second):
    whole = pl.BlockSpec(memory_space=pltpu.VMEM)
    return pl.pallas_call(
        merge_kernel,
        in_specs=[whole] * 2,
        out_specs=whole,
        out_shape=jax.ShapeDtypeStruct(first.shape, first.dtype),
        compiler_params=params(8),
        cost_estimate=pl.CostEstimate(flops=500_000, bytes_accessed=1_000_000, transcendentals=0),
        name="merge_shares",
    )(first, second)


def attend_kernel(kinds, last, starts, flags, *refs):
    count = len(kinds)
    refs = list(refs)
    take = lambda n: [refs.pop(0) for _ in range(n)]
    queries, slots = take(PLANE), take(count)
    before = take(PLANE + 1) if last else None
    outs = take(PLANE) if last else take(PLANE + 1)
    piece_of = lax.broadcasted_iota(jnp.int32, (1, count * WINDOW), 1) // PIECE
    ones = jnp.ones((count * WINDOW, HEAD_DIM), jnp.bfloat16)
    level_ref = refs.pop(0) if last else outs[PLANE]
    level_ref[...] = jnp.zeros_like(level_ref)
    for c in range(TILE_COLS):
        here = slice(c * PIECE, (c + 1) * PIECE)
        window = pl.ds(pl.multiple_of(starts[c] * PIECE, PIECE), WINDOW)
        bias = jnp.full((1, count * WINDOW), -jnp.inf, jnp.float32)
        for n in range(3 * count):
            bias = jnp.where((piece_of == n) & (flags[c, kinds[n // 3] * 3 + n % 3] > 0), 0.0, bias)
        for h in range(HEADS_HERE):
            head = slice(h * HEAD_DIM, (h + 1) * HEAD_DIM)
            value_head = slice(WIDTH + h * HEAD_DIM, WIDTH + (h + 1) * HEAD_DIM)
            lane = slice(HEADS_HERE * c + h, HEADS_HERE * c + h + 1)
            q = jnp.concatenate([ref[here, head] for ref in queries], axis=0)
            k = jnp.concatenate([slot[window, head] for slot in slots], axis=0)
            v = jnp.concatenate([slot[window, value_head] for slot in slots], axis=0)
            scores = lax.dot_general(
                q, k, (((1,), (1,)), ((), ())), preferred_element_type=jnp.float32
            )
            scores = scores * SCORE_SCALE + bias
            top = jnp.maximum(jnp.max(scores, axis=-1, keepdims=True), LOWEST)
            weights = jnp.exp2(scores - top).astype(jnp.bfloat16)
            both = jnp.dot(
                weights, jnp.concatenate([v, ones], axis=1), preferred_element_type=jnp.float32
            )
            mixed, total = both[:, :HEAD_DIM], both[:, HEAD_DIM:]
            if last:
                other = before[PLANE][:, lane]
                mixed_before = jnp.concatenate([ref[here, head] for ref in before[:PLANE]], axis=0)
                high = jnp.maximum(top, other)
                share = jnp.exp2(other - high)
                mine = jnp.exp2(top - high)
                whole = mine * total + share
                mixed = (mixed * mine + mixed_before.astype(jnp.float32) * share) / whole
                level = high + jnp.log2(whole)
            else:
                mixed = mixed / total
                level = top + jnp.log2(total)
            mixed = mixed.astype(jnp.bfloat16)
            for n in range(PLANE):
                outs[n][here, head] = mixed[n * PIECE : (n + 1) * PIECE]
            level_ref[:, lane] = level[:, lane]
    if last:
        for n in range(PLANE):
            store_level(outs[n], level_ref[n * PIECE : (n + 1) * PIECE])


def attend(starts, flags, queries, slots, kinds, before=()):
    tokens = TILE_COLS * PIECE
    count = len(slots)
    last = bool(before)
    whole = pl.BlockSpec(memory_space=pltpu.VMEM)
    scalars = pl.BlockSpec(memory_space=pltpu.SMEM)
    operands = [*queries, *slots, *before]
    levels = (PLANE * PIECE, HEAD_DIM)
    if last:
        out_shape = [jax.ShapeDtypeStruct((tokens + PIECE, WIDTH), jnp.bfloat16)] * PLANE
    else:
        out_shape = [jax.ShapeDtypeStruct((tokens, WIDTH), jnp.bfloat16)] * PLANE
        out_shape.append(jax.ShapeDtypeStruct(levels, jnp.float32))
    scratch = [pltpu.VMEM(levels, jnp.float32)] if last else []
    return pl.pallas_call(
        functools.partial(attend_kernel, kinds, last),
        in_specs=[scalars] * 2 + [whole] * len(operands),
        out_specs=[whole] * len(out_shape),
        out_shape=out_shape,
        scratch_shapes=scratch,
        compiler_params=params(16),
        cost_estimate=pl.CostEstimate(
            flops=4 * PLANE * tokens * count * WINDOW * WIDTH,
            bytes_accessed=4_000_000,
            transcendentals=1_000_000,
        ),
        name="attend",
    )(starts, flags, *operands)


def term(ids, k, attended, w_ref, out_ref):
    columns = pl.ds(pl.multiple_of((ids[1] ^ k) * WIDTH, WIDTH), WIDTH)
    out_ref[...] = jnp.dot(
        attended, w_ref[:, columns], preferred_element_type=jnp.float32
    ).astype(jnp.bfloat16)


def join_kernel(ids, *refs):
    *shares, w_ref, joined = refs[: -len(RELAYED)]
    merge(shares, joined)
    for k, out_ref in zip(RELAYED, refs[-len(RELAYED) :]):
        term(ids, k, joined[...], w_ref, out_ref)


def join(ids, shares, w_out):
    tokens = TILE_COLS * PIECE
    whole = pl.BlockSpec(memory_space=pltpu.VMEM)
    return pl.pallas_call(
        join_kernel,
        in_specs=[pl.BlockSpec(memory_space=pltpu.SMEM)] + [whole] * (len(shares) + 1),
        out_specs=[whole] * (1 + len(RELAYED)),
        out_shape=[jax.ShapeDtypeStruct((tokens, WIDTH), jnp.bfloat16)] * (1 + len(RELAYED)),
        compiler_params=params(16),
        cost_estimate=pl.CostEstimate(
            flops=2 * tokens * WIDTH * WIDTH * len(RELAYED), bytes_accessed=3_000_000, transcendentals=0
        ),
        name="join",
    )(ids, *shares, w_out)


def terms_kernel(ids, joined, w_ref, *outs):
    for k, out_ref in zip(DIRECT, outs):
        term(ids, k, joined[...], w_ref, out_ref)


def direct_terms(ids, joined, w_out):
    whole = pl.BlockSpec(memory_space=pltpu.VMEM)
    return pl.pallas_call(
        terms_kernel,
        in_specs=[pl.BlockSpec(memory_space=pltpu.SMEM)] + [whole] * 2,
        out_specs=[whole] * len(DIRECT),
        out_shape=[jax.ShapeDtypeStruct(joined.shape, jnp.bfloat16)] * len(DIRECT),
        compiler_params=params(16),
        cost_estimate=pl.CostEstimate(
            flops=2 * joined.size * WIDTH * len(DIRECT), bytes_accessed=4_000_000, transcendentals=0
        ),
        name="direct_terms",
    )(ids, joined, w_out)


def add_kernel(side, *refs):
    *terms, kept_ref, given_ref, rows = refs
    total = terms[0][...].astype(jnp.float32)
    for ref in terms[1:]:
        total = total + ref[...].astype(jnp.float32)
    rows[...] = total.astype(jnp.bfloat16)
    for c in range(TILE_COLS):
        to = slice(c * PAIR, (c + 1) * PAIR)
        for ref, which in ((kept_ref, side[0]), (given_ref, 1 - side[0])):
            start = pl.multiple_of(c * PIECE + which * PAIR, PAIR)
            ref[to, :] = rows[pl.ds(start, PAIR), :]


def add_terms(side, terms):
    whole = pl.BlockSpec(memory_space=pltpu.VMEM)
    return pl.pallas_call(
        add_kernel,
        in_specs=[pl.BlockSpec(memory_space=pltpu.SMEM)] + [whole] * len(terms),
        out_specs=[whole] * 2,
        out_shape=[jax.ShapeDtypeStruct((TILE_COLS * PAIR, WIDTH), jnp.bfloat16)] * 2,
        scratch_shapes=[pltpu.VMEM((TILE_COLS * PIECE, WIDTH), jnp.bfloat16)],
        compiler_params=params(8),
        cost_estimate=pl.CostEstimate(flops=800_000, bytes_accessed=2_000_000, transcendentals=0),
        name="add_terms",
    )(side, *terms)


def order_kernel(side, tile_of, kept_ref, got_ref, out_ref, rows):
    size = TILE_COLS * PAIR
    for ref, which in ((kept_ref, side[0]), (got_ref, 1 - side[0])):
        rows[pl.ds(pl.multiple_of(which * size, size), size), :] = ref[...]
    for d in range(TILES):
        start = pl.multiple_of((tile_of[d] % (2 * TILE_COLS)) * PAIR, PAIR)
        out_ref[d * PAIR : (d + 1) * PAIR, :] = rows[pl.ds(start, PAIR), :]


def order(side, tile_of, kept, got):
    whole = pl.BlockSpec(memory_space=pltpu.VMEM)
    scalars = pl.BlockSpec(memory_space=pltpu.SMEM)
    return pl.pallas_call(
        order_kernel,
        in_specs=[scalars, scalars, whole, whole],
        out_specs=whole,
        out_shape=jax.ShapeDtypeStruct((TILES * PAIR, WIDTH), jnp.bfloat16),
        scratch_shapes=[pltpu.VMEM((2 * TILE_COLS * PAIR, WIDTH), jnp.bfloat16)],
        compiler_params=params(8),
        cost_estimate=pl.CostEstimate(flops=100_000, bytes_accessed=800_000, transcendentals=0),
        name="order",
    )(side, tile_of, kept, got)


def tile_kernel(first, arrived, out_ref):
    base = first[0] * (2 * TILE * PAIR)
    pieces = [
        arrived[pl.ds(pl.multiple_of(base + n * PAIR, PAIR), PAIR), :].astype(jnp.float32)
        for n in range(2 * TILE)
    ]
    parts = [
        pieces[(f // 2) * TILE + j][(f % 2) * TILE : (f % 2 + 1) * TILE]
        for f in range(FRAMES)
        for j in range(TILE)
    ]
    out_ref[...] = jnp.concatenate(parts, axis=0).astype(jnp.bfloat16)


def to_tile(first, arrived):
    whole = pl.BlockSpec(memory_space=pltpu.VMEM)
    return pl.pallas_call(
        tile_kernel,
        in_specs=[pl.BlockSpec(memory_space=pltpu.SMEM), whole],
        out_specs=whole,
        out_shape=jax.ShapeDtypeStruct((TILE_TOKENS, WIDTH), jnp.bfloat16),
        compiler_params=params(8),
        cost_estimate=pl.CostEstimate(flops=100_000, bytes_accessed=800_000, transcendentals=0),
        name="to_tile",
    )(first, arrived)


def head_swap(array, k):
    return lax.ppermute(array, "head", [(h, h ^ k) for h in range(N_HEAD)])


def plane_swap(array, k):
    return lax.ppermute(array, "seq", [(s, s ^ k) for s in range(PLANE * PLANES)])


def mate_swap(array):
    return plane_swap(array, PLANE)


def edge_swap(array):
    pairs = []
    for z in range(1, PLANES - 1, 2):
        for i in range(PLANE):
            pairs += [(z * PLANE + i, (z + 1) * PLANE + i), ((z + 1) * PLANE + i, z * PLANE + i)]
    return lax.ppermute(array, "seq", pairs)


def local(latent, w_qkv, q_gain, k_gain, w_out, neighbours, tile_owner):
    ids = jnp.stack([lax.axis_index("seq"), lax.axis_index("head")]).astype(jnp.int32)
    weight = load_weight(jnp.transpose(w_qkv, (1, 0, 2)))
    q_gain, k_gain = q_gain.reshape(1, HEAD_DIM), k_gain.reshape(1, HEAD_DIM)
    starts, flags, tile_of, first, half = plan(ids, neighbours.T, tile_owner)

    pieces = [latent.reshape(PIECE, D)] * N_HEAD
    for k in (1, 2, 3, 6, 7):
        pieces[k] = head_swap(pieces[0], k)
    pieces[4], pieces[5] = head_swap(pieces[6], 2), head_swap(pieces[3], 6)

    tables = (starts, flags, tile_of, first, half)
    (starts, flags, tile_of, first, half), pieces = lax.optimization_barrier((tables, pieces))

    queries, rows = project_queries(ids, pieces, weight, q_gain)
    all_queries = [queries] + [plane_swap(queries, k) for k in range(1, PLANE)]
    own = project_keys(rows, weight, k_gain)
    mate, edge = mate_swap(own), edge_swap(own)
    mate, edge, *all_queries = lax.optimization_barrier((mate, edge, *all_queries))
    far_1, edge_2 = mate_swap(edge), edge_swap(mate)
    far_2 = mate_swap(edge_2)
    near = attend(starts, flags, all_queries, [own, mate, edge], (0, 0, 1))
    shares = attend(starts, flags, all_queries, [edge_2, far_1, far_2], (1, 2, 2), near)
    from_core, for_chip = plane_swap(shares[1], 1), plane_swap(shares[3], 1)
    from_chip = plane_swap(merge_shares(shares[2], for_chip), 2)

    joined, *relayed = join(ids, [shares[0], from_core, from_chip], w_out)
    passed = {6: head_swap(relayed[0], 2), 3: head_swap(relayed[1], 6)}
    terms = dict(zip(DIRECT, direct_terms(ids, joined, w_out)))
    for k in (6, 3):
        terms[k] = (terms[k].astype(jnp.float32) + passed[k].astype(jnp.float32)).astype(jnp.bfloat16)
    terms = [terms[0]] + [head_swap(terms[k], k) for k in DIRECT[1:]]

    kept, given = add_terms(half, terms)
    sent = order(half, tile_of, kept, plane_swap(given, TILE))
    arrived = lax.all_to_all(
        sent.reshape(TILES, PAIR, WIDTH), "seq", split_axis=0, concat_axis=0, tiled=True
    )
    return to_tile(first, arrived.reshape(TILES * PAIR, WIDTH)).reshape(1, TILE_TOKENS, WIDTH)


def solution(mesh):
    placed = (
        P(None, "seq", "head", None),
        P(None, None, "head"),
        P(),
        P(),
        P("head", None),
        P(),
        P(),
    )
    return jax.shard_map(
        local, mesh=mesh, in_specs=placed, out_specs=P("seq", None, "head"), check_vma=False
    )
```

```python
import functools

import jax
import jax.numpy as jnp
from jax import lax
from jax.experimental import pallas as pl
from jax.experimental.pallas import tpu as pltpu
from jax.sharding import PartitionSpec as P

D = 3072
HEAD_DIM = 128
FRAMES = 4
TILE = 8
TILE_COLS = 8
TILES = 32
TILE_TOKENS = 256
N_HEAD = 8
PLANE = 4
PLANES = 8
PIECE = FRAMES * TILE
PAIR = 2 * TILE
WIDTH = 384
HEADS_HERE = 3
SLOTS = 6
WINDOW = 3 * PIECE
HALF = N_HEAD // 2
SCORE_SCALE = HEAD_DIM ** (-0.5) * 1.4426950408889634

LOADS = 4

RELAYED = (4, 5)
DIRECT = (0, 1, 2, 7, 6, 3)

epsilon = 1e-06
LOWEST = -1e30


def params(mib):
    return pltpu.CompilerParams(vmem_limit_bytes=mib * 1024 * 1024)


STARTS, FLAGS, TILE_OF, FIRST, SIDE, GROUP = 0, 8, 80, 112, 113, 114


def plan_kernel(ids, neighbours, tile_owner, table):
    position = ids[0]
    tile_row = position // TILE
    odd = (position // PLANE) % 2
    for c in range(TILE_COLS):
        tile = tile_row * TILE_COLS + c
        start = jnp.minimum(neighbours[0, tile] % TILE_COLS, TILE_COLS - 3)
        table[STARTS + c] = start
        for n in range(9):
            table[FLAGS + 9 * c + n] = 0
        for n in range(9):
            listed = neighbours[n, tile]

            @pl.when(listed >= 0)
            def _():
                step = listed // TILE_COLS - tile_row
                kind = jnp.where(step == 0, 0, jnp.where((step > 0) == (odd == 1), 1, 2))
                table[FLAGS + 9 * c + kind * 3 + listed % TILE_COLS - start] = 1

    for t in range(TILES):
        table[TILE_OF + tile_owner[t]] = t
    table[FIRST] = table[TILE_OF + position] // (2 * TILE_COLS)
    table[SIDE] = tile_row % 2
    table[GROUP] = ids[1]


def plan(ids, neighbours, tile_owner):
    scalars = pl.BlockSpec(memory_space=pltpu.SMEM)
    return pl.pallas_call(
        plan_kernel,
        in_specs=[scalars] * 3,
        out_specs=scalars,
        out_shape=jax.ShapeDtypeStruct((128,), jnp.int32),
        compiler_params=params(8),
        cost_estimate=pl.CostEstimate(flops=0, bytes_accessed=8_000_000, transcendentals=0),
        name="plan",
    )(ids, neighbours, tile_owner)


def normed(result, gain):
    heads = []
    for h in range(HEADS_HERE):
        part = result[:, h * HEAD_DIM : (h + 1) * HEAD_DIM]
        mean = jnp.mean(part * part, axis=-1, keepdims=True)
        heads.append((part * lax.rsqrt(mean + epsilon) * gain).astype(jnp.bfloat16))
    return jnp.concatenate(heads, axis=1)


def gather_rows(ids, steps, pieces, rows):
    count = len(pieces)
    for k, piece in zip(steps, pieces):
        start = pl.multiple_of(((ids[1] ^ k) % count) * PIECE, PIECE)
        rows[pl.ds(start, PIECE), :] = piece[...]


def load_kernel(w_ref, out_ref, sems):
    rows = D // LOADS
    copies = []
    for n in range(3):
        for e in range(LOADS):
            part = pl.ds(e * rows, rows)
            copies.append(
                pltpu.make_async_copy(w_ref.at[n, part], out_ref.at[n, part], sems.at[n, e])
            )
    for copy in copies:
        copy.start()
    for copy in copies:
        copy.wait()


def load_weight(weight):
    return pl.pallas_call(
        load_kernel,
        in_specs=[pl.BlockSpec(memory_space=pltpu.HBM)],
        out_specs=pl.BlockSpec(memory_space=pltpu.VMEM),
        out_shape=jax.ShapeDtypeStruct(weight.shape, weight.dtype),
        scratch_shapes=[pltpu.SemaphoreType.DMA((3, LOADS))],
        compiler_params=params(8),
        cost_estimate=pl.CostEstimate(flops=0, bytes_accessed=7_100_000, transcendentals=0),
        name="load_weight",
    )(weight)


def queries_kernel(ids, *refs):
    pieces, (w_ref, gain_ref, out_ref, rows_ref) = refs[:N_HEAD], refs[N_HEAD:]
    gather_rows(ids, range(N_HEAD), pieces, rows_ref)
    result = jnp.dot(rows_ref[...], w_ref[0], preferred_element_type=jnp.float32)
    out_ref[...] = normed(result, gain_ref[...])


def project_queries(ids, pieces, weight, gain):
    tokens = N_HEAD * PIECE
    whole = pl.BlockSpec(memory_space=pltpu.VMEM)
    return pl.pallas_call(
        queries_kernel,
        in_specs=[pl.BlockSpec(memory_space=pltpu.SMEM)] + [whole] * (N_HEAD + 2),
        out_specs=whole,
        out_shape=jax.ShapeDtypeStruct((tokens, WIDTH), jnp.bfloat16),
        scratch_shapes=[pltpu.VMEM((tokens, D), jnp.bfloat16)],
        compiler_params=params(16),
        cost_estimate=pl.CostEstimate(
            flops=2 * tokens * D * WIDTH, bytes_accessed=4_000_000, transcendentals=0
        ),
        name="project_queries",
    )(ids, *pieces, weight, gain)


def keys_kernel(steps, ids, *refs):
    pieces, (w_ref, gain_ref, out_ref, rows_ref) = refs[:HALF], refs[HALF:]
    gather_rows(ids, steps, pieces, rows_ref)
    rows = rows_ref[...]
    keys = jnp.dot(rows, w_ref[1], preferred_element_type=jnp.float32)
    out_ref[:, :WIDTH] = normed(keys, gain_ref[...])
    values = jnp.dot(rows, w_ref[2], preferred_element_type=jnp.float32)
    out_ref[:, WIDTH:] = values.astype(jnp.bfloat16)


def project_keys(steps, ids, pieces, weight, gain):
    tokens = HALF * PIECE
    whole = pl.BlockSpec(memory_space=pltpu.VMEM)
    return pl.pallas_call(
        functools.partial(keys_kernel, steps),
        in_specs=[pl.BlockSpec(memory_space=pltpu.SMEM)] + [whole] * (HALF + 2),
        out_specs=whole,
        out_shape=jax.ShapeDtypeStruct((tokens, 2 * WIDTH), jnp.bfloat16),
        scratch_shapes=[pltpu.VMEM((tokens, D), jnp.bfloat16)],
        compiler_params=params(16),
        cost_estimate=pl.CostEstimate(
            flops=2 * tokens * D * 2 * WIDTH, bytes_accessed=6_000_000, transcendentals=0
        ),
        name="project_keys",
    )(ids, *pieces, weight, gain)


TAIL = slice(TILE_COLS * PIECE, (TILE_COLS + 1) * PIECE)


def store_level(ref, level):
    for n in range(3):
        rounded = level.astype(jnp.bfloat16)
        level = level - rounded.astype(jnp.float32)
        ref[TAIL, n * HEAD_DIM : (n + 1) * HEAD_DIM] = rounded


def load_level(ref):
    parts = [ref[TAIL, n * HEAD_DIM : (n + 1) * HEAD_DIM].astype(jnp.float32) for n in range(3)]
    return parts[0] + (parts[1] + parts[2])


def merge(shares, out_ref):
    levels = [load_level(ref) for ref in shares]
    top = functools.reduce(jnp.maximum, levels)
    weights = [jnp.exp2(level - top) for level in levels]
    total = functools.reduce(jnp.add, weights)
    weights = [weight / total for weight in weights]
    for c in range(TILE_COLS):
        rows = slice(c * PIECE, (c + 1) * PIECE)
        for h in range(HEADS_HERE):
            head = slice(h * HEAD_DIM, (h + 1) * HEAD_DIM)
            lane = HEADS_HERE * c + h
            mixed = None
            for weight, ref in zip(weights, shares):
                term = weight[:, lane : lane + 1] * ref[rows, head].astype(jnp.float32)
                mixed = term if mixed is None else mixed + term
            out_ref[rows, head] = mixed.astype(jnp.bfloat16)
    return top + jnp.log2(total)


def merge_kernel(first_ref, second_ref, out_ref):
    store_level(out_ref, merge([first_ref, second_ref], out_ref))


def merge_shares(first, second):
    whole = pl.BlockSpec(memory_space=pltpu.VMEM)
    return pl.pallas_call(
        merge_kernel,
        in_specs=[whole] * 2,
        out_specs=whole,
        out_shape=jax.ShapeDtypeStruct(first.shape, first.dtype),
        compiler_params=params(8),
        cost_estimate=pl.CostEstimate(flops=500_000, bytes_accessed=1_000_000, transcendentals=0),
        name="merge_shares",
    )(first, second)


def attend_kernel(kinds, last, table, *refs):
    count = len(kinds)
    refs = list(refs)
    take = lambda n: [refs.pop(0) for _ in range(n)]
    queries, halves = take(PLANE), take(2 * count)
    before = take(PLANE + 1) if last else None
    outs = take(PLANE) if last else take(PLANE + 1)
    piece_of = lax.broadcasted_iota(jnp.int32, (1, count * WINDOW), 1) // PIECE
    ones = jnp.ones((count * WINDOW, HEAD_DIM), jnp.bfloat16)
    slots_ref = refs.pop(0)
    level_ref = refs.pop(0) if last else outs[PLANE]
    size = HALF * PIECE
    for n in range(count):
        for e in range(2):
            start = pl.multiple_of((table[GROUP] // HALF ^ e) * size, size)
            slots_ref[n, pl.ds(start, size), :] = halves[2 * n + e][...]
    slots = [slots_ref.at[n] for n in range(count)]
    level_ref[...] = jnp.zeros_like(level_ref)
    for c in range(TILE_COLS):
        here = slice(c * PIECE, (c + 1) * PIECE)
        window = pl.ds(pl.multiple_of(table[STARTS + c] * PIECE, PIECE), WINDOW)
        bias = jnp.full((1, count * WINDOW), -jnp.inf, jnp.float32)
        for n in range(3 * count):
            bias = jnp.where((piece_of == n) & (table[FLAGS + 9 * c + kinds[n // 3] * 3 + n % 3] > 0), 0.0, bias)
        for h in range(HEADS_HERE):
            head = slice(h * HEAD_DIM, (h + 1) * HEAD_DIM)
            value_head = slice(WIDTH + h * HEAD_DIM, WIDTH + (h + 1) * HEAD_DIM)
            lane = slice(HEADS_HERE * c + h, HEADS_HERE * c + h + 1)
            q = jnp.concatenate([ref[here, head] for ref in queries], axis=0)
            k = jnp.concatenate([slot[window, head] for slot in slots], axis=0)
            v = jnp.concatenate([slot[window, value_head] for slot in slots], axis=0)
            scores = lax.dot_general(
                q, k, (((1,), (1,)), ((), ())), preferred_element_type=jnp.float32
            )
            scores = scores * SCORE_SCALE + bias
            top = jnp.maximum(jnp.max(scores, axis=-1, keepdims=True), LOWEST)
            weights = jnp.exp2(scores - top).astype(jnp.bfloat16)
            both = jnp.dot(
                weights, jnp.concatenate([v, ones], axis=1), preferred_element_type=jnp.float32
            )
            mixed, total = both[:, :HEAD_DIM], both[:, HEAD_DIM:]
            if last:
                other = before[PLANE][:, lane]
                mixed_before = jnp.concatenate([ref[here, head] for ref in before[:PLANE]], axis=0)
                high = jnp.maximum(top, other)
                share = jnp.exp2(other - high)
                mine = jnp.exp2(top - high)
                whole = mine * total + share
                mixed = (mixed * mine + mixed_before.astype(jnp.float32) * share) / whole
                level = high + jnp.log2(whole)
            else:
                mixed = mixed / total
                level = top + jnp.log2(total)
            mixed = mixed.astype(jnp.bfloat16)
            for n in range(PLANE):
                outs[n][here, head] = mixed[n * PIECE : (n + 1) * PIECE]
            level_ref[:, lane] = level[:, lane]
    if last:
        for n in range(PLANE):
            store_level(outs[n], level_ref[n * PIECE : (n + 1) * PIECE])


def attend(table, queries, slots, kinds, before=()):
    tokens = TILE_COLS * PIECE
    count = len(slots)
    last = bool(before)
    whole = pl.BlockSpec(memory_space=pltpu.VMEM)
    scalars = pl.BlockSpec(memory_space=pltpu.SMEM)
    operands = [*queries, *(half for slot in slots for half in slot), *before]
    levels = (PLANE * PIECE, HEAD_DIM)
    if last:
        out_shape = [jax.ShapeDtypeStruct((tokens + PIECE, WIDTH), jnp.bfloat16)] * PLANE
    else:
        out_shape = [jax.ShapeDtypeStruct((tokens, WIDTH), jnp.bfloat16)] * PLANE
        out_shape.append(jax.ShapeDtypeStruct(levels, jnp.float32))
    scratch = [pltpu.VMEM((count, tokens, 2 * WIDTH), jnp.bfloat16)]
    if last:
        scratch.append(pltpu.VMEM(levels, jnp.float32))
    return pl.pallas_call(
        functools.partial(attend_kernel, kinds, last),
        in_specs=[scalars] + [whole] * len(operands),
        out_specs=[whole] * len(out_shape),
        out_shape=out_shape,
        scratch_shapes=scratch,
        compiler_params=params(16),
        cost_estimate=pl.CostEstimate(
            flops=4 * PLANE * tokens * count * WINDOW * WIDTH,
            bytes_accessed=4_000_000,
            transcendentals=1_000_000,
        ),
        name="attend",
    )(table, *operands)


def term(ids, k, attended, w_ref, out_ref):
    columns = pl.ds(pl.multiple_of((ids[1] ^ k) * WIDTH, WIDTH), WIDTH)
    out_ref[...] = jnp.dot(
        attended, w_ref[:, columns], preferred_element_type=jnp.float32
    ).astype(jnp.bfloat16)


def join_kernel(ids, *refs):
    *shares, w_ref, joined = refs[: -len(RELAYED)]
    merge(shares, joined)
    for k, out_ref in zip(RELAYED, refs[-len(RELAYED) :]):
        term(ids, k, joined[...], w_ref, out_ref)


def join(ids, shares, w_out):
    tokens = TILE_COLS * PIECE
    whole = pl.BlockSpec(memory_space=pltpu.VMEM)
    return pl.pallas_call(
        join_kernel,
        in_specs=[pl.BlockSpec(memory_space=pltpu.SMEM)] + [whole] * (len(shares) + 1),
        out_specs=[whole] * (1 + len(RELAYED)),
        out_shape=[jax.ShapeDtypeStruct((tokens, WIDTH), jnp.bfloat16)] * (1 + len(RELAYED)),
        compiler_params=params(16),
        cost_estimate=pl.CostEstimate(
            flops=2 * tokens * WIDTH * WIDTH * len(RELAYED), bytes_accessed=3_000_000, transcendentals=0
        ),
        name="join",
    )(ids, *shares, w_out)


def terms_kernel(ids, joined, w_ref, *outs):
    for k, out_ref in zip(DIRECT, outs):
        term(ids, k, joined[...], w_ref, out_ref)


def direct_terms(ids, joined, w_out):
    whole = pl.BlockSpec(memory_space=pltpu.VMEM)
    return pl.pallas_call(
        terms_kernel,
        in_specs=[pl.BlockSpec(memory_space=pltpu.SMEM)] + [whole] * 2,
        out_specs=[whole] * len(DIRECT),
        out_shape=[jax.ShapeDtypeStruct(joined.shape, jnp.bfloat16)] * len(DIRECT),
        compiler_params=params(16),
        cost_estimate=pl.CostEstimate(
            flops=2 * joined.size * WIDTH * len(DIRECT), bytes_accessed=4_000_000, transcendentals=0
        ),
        name="direct_terms",
    )(ids, joined, w_out)


def add_kernel(table, *refs):
    *terms, kept_ref, given_ref, rows = refs
    total = terms[0][...].astype(jnp.float32)
    for ref in terms[1:]:
        total = total + ref[...].astype(jnp.float32)
    rows[...] = total.astype(jnp.bfloat16)
    for c in range(TILE_COLS):
        to = slice(c * PAIR, (c + 1) * PAIR)
        for ref, which in ((kept_ref, table[SIDE]), (given_ref, 1 - table[SIDE])):
            start = pl.multiple_of(c * PIECE + which * PAIR, PAIR)
            ref[to, :] = rows[pl.ds(start, PAIR), :]


def add_terms(table, terms):
    whole = pl.BlockSpec(memory_space=pltpu.VMEM)
    return pl.pallas_call(
        add_kernel,
        in_specs=[pl.BlockSpec(memory_space=pltpu.SMEM)] + [whole] * len(terms),
        out_specs=[whole] * 2,
        out_shape=[jax.ShapeDtypeStruct((TILE_COLS * PAIR, WIDTH), jnp.bfloat16)] * 2,
        scratch_shapes=[pltpu.VMEM((TILE_COLS * PIECE, WIDTH), jnp.bfloat16)],
        compiler_params=params(8),
        cost_estimate=pl.CostEstimate(flops=800_000, bytes_accessed=2_000_000, transcendentals=0),
        name="add_terms",
    )(table, *terms)


def order_kernel(table, kept_ref, got_ref, out_ref, rows):
    size = TILE_COLS * PAIR
    for ref, which in ((kept_ref, table[SIDE]), (got_ref, 1 - table[SIDE])):
        rows[pl.ds(pl.multiple_of(which * size, size), size), :] = ref[...]
    for d in range(TILES):
        start = pl.multiple_of((table[TILE_OF + d] % (2 * TILE_COLS)) * PAIR, PAIR)
        out_ref[d * PAIR : (d + 1) * PAIR, :] = rows[pl.ds(start, PAIR), :]


def order(table, kept, got):
    whole = pl.BlockSpec(memory_space=pltpu.VMEM)
    scalars = pl.BlockSpec(memory_space=pltpu.SMEM)
    return pl.pallas_call(
        order_kernel,
        in_specs=[scalars, whole, whole],
        out_specs=whole,
        out_shape=jax.ShapeDtypeStruct((TILES * PAIR, WIDTH), jnp.bfloat16),
        scratch_shapes=[pltpu.VMEM((2 * TILE_COLS * PAIR, WIDTH), jnp.bfloat16)],
        compiler_params=params(8),
        cost_estimate=pl.CostEstimate(flops=100_000, bytes_accessed=800_000, transcendentals=0),
        name="order",
    )(table, kept, got)


def tile_kernel(table, arrived, out_ref):
    base = table[FIRST] * (2 * TILE * PAIR)
    pieces = [
        arrived[pl.ds(pl.multiple_of(base + n * PAIR, PAIR), PAIR), :].astype(jnp.float32)
        for n in range(2 * TILE)
    ]
    parts = [
        pieces[(f // 2) * TILE + j][(f % 2) * TILE : (f % 2 + 1) * TILE]
        for f in range(FRAMES)
        for j in range(TILE)
    ]
    out_ref[...] = jnp.concatenate(parts, axis=0).astype(jnp.bfloat16)


def to_tile(table, arrived):
    whole = pl.BlockSpec(memory_space=pltpu.VMEM)
    return pl.pallas_call(
        tile_kernel,
        in_specs=[pl.BlockSpec(memory_space=pltpu.SMEM), whole],
        out_specs=whole,
        out_shape=jax.ShapeDtypeStruct((TILE_TOKENS, WIDTH), jnp.bfloat16),
        compiler_params=params(8),
        cost_estimate=pl.CostEstimate(flops=100_000, bytes_accessed=800_000, transcendentals=0),
        name="to_tile",
    )(table, arrived)


def head_swap(array, k):
    return lax.ppermute(array, "head", [(h, h ^ k) for h in range(N_HEAD)])


def plane_swap(array, k):
    return lax.ppermute(array, "seq", [(s, s ^ k) for s in range(PLANE * PLANES)])


def mate_swap(array):
    return plane_swap(array, PLANE)


def edge_swap(array):
    pairs = []
    for z in range(1, PLANES - 1, 2):
        for i in range(PLANE):
            pairs += [(z * PLANE + i, (z + 1) * PLANE + i), ((z + 1) * PLANE + i, z * PLANE + i)]
    return lax.ppermute(array, "seq", pairs)


def local(latent, w_qkv, q_gain, k_gain, w_out, neighbours, tile_owner):
    ids = jnp.stack([lax.axis_index("seq"), lax.axis_index("head")]).astype(jnp.int32)
    weight = load_weight(jnp.transpose(w_qkv, (1, 0, 2)))
    q_gain, k_gain = q_gain.reshape(1, HEAD_DIM), k_gain.reshape(1, HEAD_DIM)
    table = plan(ids, neighbours.T, tile_owner)

    pieces = [latent.reshape(PIECE, D)] * N_HEAD
    for k in (1, 2, 3, 6, 7):
        pieces[k] = head_swap(pieces[0], k)
    pieces[4], pieces[5] = head_swap(pieces[6], 2), head_swap(pieces[3], 6)

    own_a = project_keys(range(HALF), ids, pieces[:HALF], weight, k_gain)
    mate_a, edge_a = mate_swap(own_a), edge_swap(own_a)
    pieces_b, _own = lax.optimization_barrier((pieces[HALF:], own_a))
    own_b = project_keys(range(HALF, N_HEAD), ids, pieces_b, weight, k_gain)
    mate_b, edge_b = mate_swap(own_b), edge_swap(own_b)
    edge_2a, far_1a = edge_swap(mate_a), mate_swap(edge_a)

    queries = project_queries(ids, [*pieces[:HALF], *pieces_b], weight, q_gain)
    q_chip = plane_swap(queries, 2)
    all_queries = [queries, plane_swap(queries, 1), q_chip, plane_swap(q_chip, 1)]

    edge_b, edge_2a, all_queries = lax.optimization_barrier((edge_b, edge_2a, all_queries))
    edge_2b = edge_swap(mate_b)
    far_1b, far_2a = mate_swap(edge_b), mate_swap(edge_2a)
    far_2b = mate_swap(edge_2b)
    near_slots = [(_own, own_b), (mate_a, mate_b), (edge_a, edge_b)]
    far_slots = [(edge_2a, edge_2b), (far_1a, far_1b), (far_2a, far_2b)]
    near = attend(table, all_queries, near_slots, (0, 0, 1))
    shares = attend(table, all_queries, far_slots, (1, 2, 2), near)

    from_core, for_chip = plane_swap(shares[1], 1), plane_swap(shares[3], 1)
    from_chip = plane_swap(merge_shares(shares[2], for_chip), 2)

    joined, *relayed = join(ids, [shares[0], from_core, from_chip], w_out)
    passed = {6: head_swap(relayed[0], 2), 3: head_swap(relayed[1], 6)}
    terms = dict(zip(DIRECT, direct_terms(ids, joined, w_out)))
    for k in (6, 3):
        terms[k] = (terms[k].astype(jnp.float32) + passed[k].astype(jnp.float32)).astype(jnp.bfloat16)
    terms = [terms[0]] + [head_swap(terms[k], k) for k in DIRECT[1:]]

    kept, given = add_terms(table, terms)
    sent = order(table, kept, plane_swap(given, TILE))
    arrived = lax.all_to_all(
        sent.reshape(TILES, PAIR, WIDTH), "seq", split_axis=0, concat_axis=0, tiled=True
    )
    return to_tile(table, arrived.reshape(TILES * PAIR, WIDTH)).reshape(1, TILE_TOKENS, WIDTH)


def solution(mesh):
    placed = (
        P(None, "seq", "head", None),
        P(None, None, "head"),
        P(),
        P(),
        P("head", None),
        P(),
        P(),
    )
    return jax.shard_map(
        local, mesh=mesh, in_specs=placed, out_specs=P("seq", None, "head"), check_vma=False
    )
```

```python
import functools

import jax
import jax.numpy as jnp
from jax import lax
from jax.experimental import pallas as pl
from jax.experimental.pallas import tpu as pltpu
from jax.sharding import PartitionSpec as P

D = 3072
HEAD_DIM = 128
FRAMES = 4
TILE = 8
TILE_COLS = 8
TILES = 32
TILE_TOKENS = 256
N_HEAD = 8
PLANE = 4
PLANES = 8
PIECE = FRAMES * TILE
PAIR = 2 * TILE
WIDTH = 384
HEADS_HERE = 3
SLOTS = 6
WINDOW = 3 * PIECE
HALF = N_HEAD // 2
SCORE_SCALE = HEAD_DIM ** (-0.5) * 1.4426950408889634

LOADS = 4

RELAYED = (4, 5)
DIRECT = (0, 1, 2, 7, 6, 3)

epsilon = 1e-06
LOWEST = -1e30


def params(mib):
    return pltpu.CompilerParams(vmem_limit_bytes=mib * 1024 * 1024)


STARTS, FLAGS, TILE_OF, FIRST, SIDE, GROUP = 0, 8, 80, 112, 113, 114


def plan_kernel(ids, neighbours, tile_owner, table):
    position = ids[0]
    tile_row = position // TILE
    odd = (position // PLANE) % 2
    for c in range(TILE_COLS):
        tile = tile_row * TILE_COLS + c
        start = jnp.minimum(neighbours[0, tile] % TILE_COLS, TILE_COLS - 3)
        table[STARTS + c] = start
        for n in range(9):
            table[FLAGS + 9 * c + n] = 0
        for n in range(9):
            listed = neighbours[n, tile]

            @pl.when(listed >= 0)
            def _():
                step = listed // TILE_COLS - tile_row
                kind = jnp.where(step == 0, 0, jnp.where((step > 0) == (odd == 1), 1, 2))
                table[FLAGS + 9 * c + kind * 3 + listed % TILE_COLS - start] = 1

    for t in range(TILES):
        table[TILE_OF + tile_owner[t]] = t
    table[FIRST] = table[TILE_OF + position] // (2 * TILE_COLS)
    table[SIDE] = tile_row % 2
    table[GROUP] = ids[1]


def plan(ids, neighbours, tile_owner):
    scalars = pl.BlockSpec(memory_space=pltpu.SMEM)
    return pl.pallas_call(
        plan_kernel,
        in_specs=[scalars] * 3,
        out_specs=scalars,
        out_shape=jax.ShapeDtypeStruct((128,), jnp.int32),
        compiler_params=params(8),
        cost_estimate=pl.CostEstimate(flops=0, bytes_accessed=8_000_000, transcendentals=0),
        name="plan",
    )(ids, neighbours, tile_owner)


def normed(result, gain):
    heads = []
    for h in range(HEADS_HERE):
        part = result[:, h * HEAD_DIM : (h + 1) * HEAD_DIM]
        mean = jnp.mean(part * part, axis=-1, keepdims=True)
        heads.append((part * lax.rsqrt(mean + epsilon) * gain).astype(jnp.bfloat16))
    return jnp.concatenate(heads, axis=1)


def gather_rows(ids, steps, pieces, rows):
    count = len(pieces)
    for k, piece in zip(steps, pieces):
        start = pl.multiple_of(((ids[1] ^ k) % count) * PIECE, PIECE)
        rows[pl.ds(start, PIECE), :] = piece[...]


def load_kernel(w_ref, out_ref, sems):
    rows = D // LOADS
    copies = []
    for n in range(3):
        for e in range(LOADS):
            part = pl.ds(e * rows, rows)
            copies.append(
                pltpu.make_async_copy(w_ref.at[n, part], out_ref.at[n, part], sems.at[n, e])
            )
    for copy in copies:
        copy.start()
    for copy in copies:
        copy.wait()


def load_weight(weight):
    return pl.pallas_call(
        load_kernel,
        in_specs=[pl.BlockSpec(memory_space=pltpu.HBM)],
        out_specs=pl.BlockSpec(memory_space=pltpu.VMEM),
        out_shape=jax.ShapeDtypeStruct(weight.shape, weight.dtype),
        scratch_shapes=[pltpu.SemaphoreType.DMA((3, LOADS))],
        compiler_params=params(8),
        cost_estimate=pl.CostEstimate(flops=0, bytes_accessed=7_100_000, transcendentals=0),
        name="load_weight",
    )(weight)


def queries_kernel(ids, *refs):
    pieces, (w_ref, gain_ref, out_ref, rows_ref) = refs[:N_HEAD], refs[N_HEAD:]
    gather_rows(ids, range(N_HEAD), pieces, rows_ref)
    result = jnp.dot(rows_ref[...], w_ref[0], preferred_element_type=jnp.float32)
    out_ref[...] = normed(result, gain_ref[...])


def project_queries(ids, pieces, weight, gain):
    tokens = N_HEAD * PIECE
    whole = pl.BlockSpec(memory_space=pltpu.VMEM)
    return pl.pallas_call(
        queries_kernel,
        in_specs=[pl.BlockSpec(memory_space=pltpu.SMEM)] + [whole] * (N_HEAD + 2),
        out_specs=whole,
        out_shape=jax.ShapeDtypeStruct((tokens, WIDTH), jnp.bfloat16),
        scratch_shapes=[pltpu.VMEM((tokens, D), jnp.bfloat16)],
        compiler_params=params(16),
        cost_estimate=pl.CostEstimate(
            flops=2 * tokens * D * WIDTH, bytes_accessed=4_000_000, transcendentals=0
        ),
        name="project_queries",
    )(ids, *pieces, weight, gain)


def keys_kernel(steps, ids, *refs):
    pieces, (w_ref, gain_ref, out_ref, rows_ref) = refs[:HALF], refs[HALF:]
    gather_rows(ids, steps, pieces, rows_ref)
    rows = rows_ref[...]
    keys = jnp.dot(rows, w_ref[1], preferred_element_type=jnp.float32)
    out_ref[:, :WIDTH] = normed(keys, gain_ref[...])
    values = jnp.dot(rows, w_ref[2], preferred_element_type=jnp.float32)
    out_ref[:, WIDTH:] = values.astype(jnp.bfloat16)


def project_keys(steps, ids, pieces, weight, gain):
    tokens = HALF * PIECE
    whole = pl.BlockSpec(memory_space=pltpu.VMEM)
    return pl.pallas_call(
        functools.partial(keys_kernel, steps),
        in_specs=[pl.BlockSpec(memory_space=pltpu.SMEM)] + [whole] * (HALF + 2),
        out_specs=whole,
        out_shape=jax.ShapeDtypeStruct((tokens, 2 * WIDTH), jnp.bfloat16),
        scratch_shapes=[pltpu.VMEM((tokens, D), jnp.bfloat16)],
        compiler_params=params(16),
        cost_estimate=pl.CostEstimate(
            flops=2 * tokens * D * 2 * WIDTH, bytes_accessed=6_000_000, transcendentals=0
        ),
        name="project_keys",
    )(ids, *pieces, weight, gain)


TAIL = slice(TILE_COLS * PIECE, (TILE_COLS + 1) * PIECE)


def store_level(ref, level):
    for n in range(3):
        rounded = level.astype(jnp.bfloat16)
        level = level - rounded.astype(jnp.float32)
        ref[TAIL, n * HEAD_DIM : (n + 1) * HEAD_DIM] = rounded


def load_level(ref):
    parts = [ref[TAIL, n * HEAD_DIM : (n + 1) * HEAD_DIM].astype(jnp.float32) for n in range(3)]
    return parts[0] + (parts[1] + parts[2])


def merge(shares, out_ref):
    levels = [load_level(ref) for ref in shares]
    top = functools.reduce(jnp.maximum, levels)
    weights = [jnp.exp2(level - top) for level in levels]
    total = functools.reduce(jnp.add, weights)
    weights = [weight / total for weight in weights]
    for c in range(TILE_COLS):
        rows = slice(c * PIECE, (c + 1) * PIECE)
        for h in range(HEADS_HERE):
            head = slice(h * HEAD_DIM, (h + 1) * HEAD_DIM)
            lane = HEADS_HERE * c + h
            mixed = None
            for weight, ref in zip(weights, shares):
                term = weight[:, lane : lane + 1] * ref[rows, head].astype(jnp.float32)
                mixed = term if mixed is None else mixed + term
            out_ref[rows, head] = mixed.astype(jnp.bfloat16)
    return top + jnp.log2(total)


def merge_kernel(*refs):
    *shares, out_ref = refs
    store_level(out_ref, merge(shares, out_ref))


def merge_shares(*shares):
    whole = pl.BlockSpec(memory_space=pltpu.VMEM)
    return pl.pallas_call(
        merge_kernel,
        in_specs=[whole] * len(shares),
        out_specs=whole,
        out_shape=jax.ShapeDtypeStruct(shares[0].shape, shares[0].dtype),
        compiler_params=params(8),
        cost_estimate=pl.CostEstimate(flops=500_000, bytes_accessed=1_000_000, transcendentals=0),
        name="merge_shares",
    )(*shares)


def attend_kernel(kinds, table, *refs):
    count = len(kinds)
    refs = list(refs)
    take = lambda n: [refs.pop(0) for _ in range(n)]
    queries, halves = take(PLANE), take(2 * count)
    outs = take(PLANE)
    piece_of = lax.broadcasted_iota(jnp.int32, (1, count * WINDOW), 1) // PIECE
    ones = jnp.ones((count * WINDOW, HEAD_DIM), jnp.bfloat16)
    slots_ref = refs.pop(0)
    level_ref = refs.pop(0)
    size = HALF * PIECE
    for n in range(count):
        for e in range(2):
            start = pl.multiple_of((table[GROUP] // HALF ^ e) * size, size)
            slots_ref[n, pl.ds(start, size), :] = halves[2 * n + e][...]
    slots = [slots_ref.at[n] for n in range(count)]
    level_ref[...] = jnp.zeros_like(level_ref)
    for c in range(TILE_COLS):
        here = slice(c * PIECE, (c + 1) * PIECE)
        window = pl.ds(pl.multiple_of(table[STARTS + c] * PIECE, PIECE), WINDOW)
        bias = jnp.full((1, count * WINDOW), -jnp.inf, jnp.float32)
        for n in range(3 * count):
            bias = jnp.where((piece_of == n) & (table[FLAGS + 9 * c + kinds[n // 3] * 3 + n % 3] > 0), 0.0, bias)
        for h in range(HEADS_HERE):
            head = slice(h * HEAD_DIM, (h + 1) * HEAD_DIM)
            value_head = slice(WIDTH + h * HEAD_DIM, WIDTH + (h + 1) * HEAD_DIM)
            lane = slice(HEADS_HERE * c + h, HEADS_HERE * c + h + 1)
            q = jnp.concatenate([ref[here, head] for ref in queries], axis=0)
            k = jnp.concatenate([slot[window, head] for slot in slots], axis=0)
            v = jnp.concatenate([slot[window, value_head] for slot in slots], axis=0)
            scores = lax.dot_general(
                q, k, (((1,), (1,)), ((), ())), preferred_element_type=jnp.float32
            )
            scores = scores * SCORE_SCALE + bias
            top = jnp.maximum(jnp.max(scores, axis=-1, keepdims=True), LOWEST)
            weights = jnp.exp2(scores - top).astype(jnp.bfloat16)
            both = jnp.dot(
                weights, jnp.concatenate([v, ones], axis=1), preferred_element_type=jnp.float32
            )
            mixed, total = both[:, :HEAD_DIM], both[:, HEAD_DIM:]
            mixed = mixed / jnp.maximum(total, 0.5)
            level = jnp.maximum(top + jnp.log2(total), LOWEST)
            mixed = mixed.astype(jnp.bfloat16)
            for n in range(PLANE):
                outs[n][here, head] = mixed[n * PIECE : (n + 1) * PIECE]
            level_ref[:, lane] = level[:, lane]
    for n in range(PLANE):
        store_level(outs[n], level_ref[n * PIECE : (n + 1) * PIECE])


def attend(table, queries, slots, kinds):
    tokens = TILE_COLS * PIECE
    count = len(slots)
    whole = pl.BlockSpec(memory_space=pltpu.VMEM)
    scalars = pl.BlockSpec(memory_space=pltpu.SMEM)
    operands = [*queries, *(half for slot in slots for half in slot)]
    out_shape = [jax.ShapeDtypeStruct((tokens + PIECE, WIDTH), jnp.bfloat16)] * PLANE
    scratch = [
        pltpu.VMEM((count, tokens, 2 * WIDTH), jnp.bfloat16),
        pltpu.VMEM((PLANE * PIECE, HEAD_DIM), jnp.float32),
    ]
    return pl.pallas_call(
        functools.partial(attend_kernel, kinds),
        in_specs=[scalars] + [whole] * len(operands),
        out_specs=[whole] * len(out_shape),
        out_shape=out_shape,
        scratch_shapes=scratch,
        compiler_params=params(16),
        cost_estimate=pl.CostEstimate(
            flops=4 * PLANE * tokens * count * WINDOW * WIDTH,
            bytes_accessed=4_000_000,
            transcendentals=1_000_000,
        ),
        name="attend",
    )(table, *operands)


def term(ids, k, attended, w_ref, out_ref):
    columns = pl.ds(pl.multiple_of((ids[1] ^ k) * WIDTH, WIDTH), WIDTH)
    out_ref[...] = jnp.dot(
        attended, w_ref[:, columns], preferred_element_type=jnp.float32
    ).astype(jnp.bfloat16)


def join_kernel(ids, *refs):
    *shares, w_ref, joined = refs[: -len(RELAYED)]
    merge(shares, joined)
    for k, out_ref in zip(RELAYED, refs[-len(RELAYED) :]):
        term(ids, k, joined[...], w_ref, out_ref)


def join(ids, shares, w_out):
    tokens = TILE_COLS * PIECE
    whole = pl.BlockSpec(memory_space=pltpu.VMEM)
    return pl.pallas_call(
        join_kernel,
        in_specs=[pl.BlockSpec(memory_space=pltpu.SMEM)] + [whole] * (len(shares) + 1),
        out_specs=[whole] * (1 + len(RELAYED)),
        out_shape=[jax.ShapeDtypeStruct((tokens, WIDTH), jnp.bfloat16)] * (1 + len(RELAYED)),
        compiler_params=params(16),
        cost_estimate=pl.CostEstimate(
            flops=2 * tokens * WIDTH * WIDTH * len(RELAYED), bytes_accessed=3_000_000, transcendentals=0
        ),
        name="join",
    )(ids, *shares, w_out)


def terms_kernel(ids, joined, w_ref, *outs):
    for k, out_ref in zip(DIRECT, outs):
        term(ids, k, joined[...], w_ref, out_ref)


def direct_terms(ids, joined, w_out):
    whole = pl.BlockSpec(memory_space=pltpu.VMEM)
    return pl.pallas_call(
        terms_kernel,
        in_specs=[pl.BlockSpec(memory_space=pltpu.SMEM)] + [whole] * 2,
        out_specs=[whole] * len(DIRECT),
        out_shape=[jax.ShapeDtypeStruct(joined.shape, jnp.bfloat16)] * len(DIRECT),
        compiler_params=params(16),
        cost_estimate=pl.CostEstimate(
            flops=2 * joined.size * WIDTH * len(DIRECT), bytes_accessed=4_000_000, transcendentals=0
        ),
        name="direct_terms",
    )(ids, joined, w_out)


def add_kernel(table, *refs):
    *terms, kept_ref, given_ref, rows = refs
    total = terms[0][...].astype(jnp.float32)
    for ref in terms[1:]:
        total = total + ref[...].astype(jnp.float32)
    rows[...] = total.astype(jnp.bfloat16)
    for c in range(TILE_COLS):
        to = slice(c * PAIR, (c + 1) * PAIR)
        for ref, which in ((kept_ref, table[SIDE]), (given_ref, 1 - table[SIDE])):
            start = pl.multiple_of(c * PIECE + which * PAIR, PAIR)
            ref[to, :] = rows[pl.ds(start, PAIR), :]


def add_terms(table, terms):
    whole = pl.BlockSpec(memory_space=pltpu.VMEM)
    return pl.pallas_call(
        add_kernel,
        in_specs=[pl.BlockSpec(memory_space=pltpu.SMEM)] + [whole] * len(terms),
        out_specs=[whole] * 2,
        out_shape=[jax.ShapeDtypeStruct((TILE_COLS * PAIR, WIDTH), jnp.bfloat16)] * 2,
        scratch_shapes=[pltpu.VMEM((TILE_COLS * PIECE, WIDTH), jnp.bfloat16)],
        compiler_params=params(8),
        cost_estimate=pl.CostEstimate(flops=800_000, bytes_accessed=2_000_000, transcendentals=0),
        name="add_terms",
    )(table, *terms)


def order_kernel(table, kept_ref, got_ref, out_ref, rows):
    size = TILE_COLS * PAIR
    for ref, which in ((kept_ref, table[SIDE]), (got_ref, 1 - table[SIDE])):
        rows[pl.ds(pl.multiple_of(which * size, size), size), :] = ref[...]
    for d in range(TILES):
        start = pl.multiple_of((table[TILE_OF + d] % (2 * TILE_COLS)) * PAIR, PAIR)
        out_ref[d * PAIR : (d + 1) * PAIR, :] = rows[pl.ds(start, PAIR), :]


def order(table, kept, got):
    whole = pl.BlockSpec(memory_space=pltpu.VMEM)
    scalars = pl.BlockSpec(memory_space=pltpu.SMEM)
    return pl.pallas_call(
        order_kernel,
        in_specs=[scalars, whole, whole],
        out_specs=whole,
        out_shape=jax.ShapeDtypeStruct((TILES * PAIR, WIDTH), jnp.bfloat16),
        scratch_shapes=[pltpu.VMEM((2 * TILE_COLS * PAIR, WIDTH), jnp.bfloat16)],
        compiler_params=params(8),
        cost_estimate=pl.CostEstimate(flops=100_000, bytes_accessed=800_000, transcendentals=0),
        name="order",
    )(table, kept, got)


def tile_kernel(table, arrived, out_ref):
    base = table[FIRST] * (2 * TILE * PAIR)
    pieces = [
        arrived[pl.ds(pl.multiple_of(base + n * PAIR, PAIR), PAIR), :].astype(jnp.float32)
        for n in range(2 * TILE)
    ]
    parts = [
        pieces[(f // 2) * TILE + j][(f % 2) * TILE : (f % 2 + 1) * TILE]
        for f in range(FRAMES)
        for j in range(TILE)
    ]
    out_ref[...] = jnp.concatenate(parts, axis=0).astype(jnp.bfloat16)


def to_tile(table, arrived):
    whole = pl.BlockSpec(memory_space=pltpu.VMEM)
    return pl.pallas_call(
        tile_kernel,
        in_specs=[pl.BlockSpec(memory_space=pltpu.SMEM), whole],
        out_specs=whole,
        out_shape=jax.ShapeDtypeStruct((TILE_TOKENS, WIDTH), jnp.bfloat16),
        compiler_params=params(8),
        cost_estimate=pl.CostEstimate(flops=100_000, bytes_accessed=800_000, transcendentals=0),
        name="to_tile",
    )(table, arrived)


def head_swap(array, k):
    return lax.ppermute(array, "head", [(h, h ^ k) for h in range(N_HEAD)])


def plane_swap(array, k):
    return lax.ppermute(array, "seq", [(s, s ^ k) for s in range(PLANE * PLANES)])


def mate_swap(array):
    return plane_swap(array, PLANE)


def edge_swap(array):
    pairs = []
    for z in range(1, PLANES - 1, 2):
        for i in range(PLANE):
            pairs += [(z * PLANE + i, (z + 1) * PLANE + i), ((z + 1) * PLANE + i, z * PLANE + i)]
    return lax.ppermute(array, "seq", pairs)


def local(latent, w_qkv, q_gain, k_gain, w_out, neighbours, tile_owner):
    ids = jnp.stack([lax.axis_index("seq"), lax.axis_index("head")]).astype(jnp.int32)
    weight = load_weight(jnp.transpose(w_qkv, (1, 0, 2)))
    q_gain, k_gain = q_gain.reshape(1, HEAD_DIM), k_gain.reshape(1, HEAD_DIM)
    table = plan(ids, neighbours.T, tile_owner)

    pieces = [latent.reshape(PIECE, D)] * N_HEAD
    for k in (1, 2, 3, 6, 7):
        pieces[k] = head_swap(pieces[0], k)
    pieces[4], pieces[5] = head_swap(pieces[6], 2), head_swap(pieces[3], 6)

    own_a = project_keys(range(HALF), ids, pieces[:HALF], weight, k_gain)
    mate_a, edge_a = mate_swap(own_a), edge_swap(own_a)
    pieces_b, _own = lax.optimization_barrier((pieces[HALF:], own_a))
    own_b = project_keys(range(HALF, N_HEAD), ids, pieces_b, weight, k_gain)
    mate_b, edge_b = mate_swap(own_b), edge_swap(own_b)
    edge_2a, far_1a = edge_swap(mate_a), mate_swap(edge_a)

    queries = project_queries(ids, [*pieces[:HALF], *pieces_b], weight, q_gain)
    q_chip = plane_swap(queries, 2)
    all_queries = [queries, plane_swap(queries, 1), q_chip, plane_swap(q_chip, 1)]

    edge_b, edge_2a, all_queries = lax.optimization_barrier((edge_b, edge_2a, all_queries))
    edge_2b = edge_swap(mate_b)
    far_1b, far_2a = mate_swap(edge_b), mate_swap(edge_2a)
    far_2b = mate_swap(edge_2b)
    near_slots = [(_own, own_b), (mate_a, mate_b), (edge_a, edge_b)]
    far_slots = [(edge_2a, edge_2b), (far_1a, far_1b), (far_2a, far_2b)]
    near = attend(table, all_queries, near_slots, (0, 0, 1))
    near_own = merge_shares(near[0], plane_swap(near[1], 1))
    near_chip = merge_shares(near[2], plane_swap(near[3], 1))
    far = attend(table, all_queries, far_slots, (1, 2, 2))
    from_core, for_chip = plane_swap(far[1], 1), plane_swap(far[3], 1)
    from_chip = plane_swap(merge_shares(near_chip, far[2], for_chip), 2)

    joined, *relayed = join(ids, [near_own, far[0], from_core, from_chip], w_out)
    passed = {6: head_swap(relayed[0], 2), 3: head_swap(relayed[1], 6)}
    terms = dict(zip(DIRECT, direct_terms(ids, joined, w_out)))
    for k in (6, 3):
        terms[k] = (terms[k].astype(jnp.float32) + passed[k].astype(jnp.float32)).astype(jnp.bfloat16)
    terms = [terms[0]] + [head_swap(terms[k], k) for k in DIRECT[1:]]

    kept, given = add_terms(table, terms)
    sent = order(table, kept, plane_swap(given, TILE))
    arrived = lax.all_to_all(
        sent.reshape(TILES, PAIR, WIDTH), "seq", split_axis=0, concat_axis=0, tiled=True
    )
    return to_tile(table, arrived.reshape(TILES * PAIR, WIDTH)).reshape(1, TILE_TOKENS, WIDTH)


def solution(mesh):
    placed = (
        P(None, "seq", "head", None),
        P(None, None, "head"),
        P(),
        P(),
        P("head", None),
        P(),
        P(),
    )
    return jax.shard_map(
        local, mesh=mesh, in_specs=placed, out_specs=P("seq", None, "head"), check_vma=False
    )
```

```python
import functools

import jax
import jax.numpy as jnp
from jax import lax
from jax.experimental import pallas as pl
from jax.experimental.pallas import tpu as pltpu
from jax.sharding import PartitionSpec as P

D = 3072
HEAD_DIM = 128
FRAMES = 4
TILE = 8
TILE_COLS = 8
TILES = 32
TILE_TOKENS = 256
N_HEAD = 8
PLANE = 4
PLANES = 8
PIECE = FRAMES * TILE
PAIR = 2 * TILE
WIDTH = 384
HEADS_HERE = 3
SLOTS = 6
WINDOW = 3 * PIECE
HALF = N_HEAD // 2
SCORE_SCALE = HEAD_DIM ** (-0.5) * 1.4426950408889634

LOADS = 4

RELAYED = (4, 5)
DIRECT = (0, 1, 2, 7, 6, 3)

epsilon = 1e-06
LOWEST = -1e30


def params(mib):
    return pltpu.CompilerParams(vmem_limit_bytes=mib * 1024 * 1024)


STARTS, FLAGS, TILE_OF, FIRST, SIDE, GROUP = 0, 8, 80, 112, 113, 114


def plan_kernel(ids, neighbours, tile_owner, table):
    position = ids[0]
    tile_row = position // TILE
    odd = (position // PLANE) % 2
    for c in range(TILE_COLS):
        tile = tile_row * TILE_COLS + c
        start = jnp.minimum(neighbours[0, tile] % TILE_COLS, TILE_COLS - 3)
        table[STARTS + c] = start
        for n in range(9):
            table[FLAGS + 9 * c + n] = 0
        for n in range(9):
            listed = neighbours[n, tile]

            @pl.when(listed >= 0)
            def _():
                step = listed // TILE_COLS - tile_row
                kind = jnp.where(step == 0, 0, jnp.where((step > 0) == (odd == 1), 1, 2))
                table[FLAGS + 9 * c + kind * 3 + listed % TILE_COLS - start] = 1

    for t in range(TILES):
        table[TILE_OF + tile_owner[t]] = t
    table[FIRST] = table[TILE_OF + position] // (2 * TILE_COLS)
    table[SIDE] = tile_row % 2
    table[GROUP] = ids[1]


def plan(ids, neighbours, tile_owner):
    scalars = pl.BlockSpec(memory_space=pltpu.SMEM)
    return pl.pallas_call(
        plan_kernel,
        in_specs=[scalars] * 3,
        out_specs=scalars,
        out_shape=jax.ShapeDtypeStruct((128,), jnp.int32),
        compiler_params=params(8),
        cost_estimate=pl.CostEstimate(flops=0, bytes_accessed=8_000_000, transcendentals=0),
        name="plan",
    )(ids, neighbours, tile_owner)


def normed(result, gain):
    heads = []
    for h in range(HEADS_HERE):
        part = result[:, h * HEAD_DIM : (h + 1) * HEAD_DIM]
        mean = jnp.mean(part * part, axis=-1, keepdims=True)
        heads.append((part * lax.rsqrt(mean + epsilon) * gain).astype(jnp.bfloat16))
    return jnp.concatenate(heads, axis=1)


def gather_rows(ids, steps, pieces, rows):
    count = len(pieces)
    for k, piece in zip(steps, pieces):
        start = pl.multiple_of(((ids[1] ^ k) % count) * PIECE, PIECE)
        rows[pl.ds(start, PIECE), :] = piece[...]


def load_kernel(w_ref, out_ref, sems):
    rows = D // LOADS
    copies = []
    for n in range(3):
        for e in range(LOADS):
            part = pl.ds(e * rows, rows)
            copies.append(
                pltpu.make_async_copy(w_ref.at[n, part], out_ref.at[n, part], sems.at[n, e])
            )
    for copy in copies:
        copy.start()
    for copy in copies:
        copy.wait()


def load_weight(weight):
    return pl.pallas_call(
        load_kernel,
        in_specs=[pl.BlockSpec(memory_space=pltpu.HBM)],
        out_specs=pl.BlockSpec(memory_space=pltpu.VMEM),
        out_shape=jax.ShapeDtypeStruct(weight.shape, weight.dtype),
        scratch_shapes=[pltpu.SemaphoreType.DMA((3, LOADS))],
        compiler_params=params(47),
        cost_estimate=pl.CostEstimate(flops=0, bytes_accessed=7_100_000, transcendentals=0),
        name="load_weight",
    )(weight)


def queries_kernel(ids, *refs):
    pieces, (w_ref, gain_ref, out_ref, rows_ref) = refs[:N_HEAD], refs[N_HEAD:]
    gather_rows(ids, range(N_HEAD), pieces, rows_ref)
    result = jnp.dot(rows_ref[...], w_ref[0], preferred_element_type=jnp.float32)
    out_ref[...] = normed(result, gain_ref[...])


def project_queries(ids, pieces, weight, gain):
    tokens = N_HEAD * PIECE
    whole = pl.BlockSpec(memory_space=pltpu.VMEM)
    return pl.pallas_call(
        queries_kernel,
        in_specs=[pl.BlockSpec(memory_space=pltpu.SMEM)] + [whole] * (N_HEAD + 2),
        out_specs=whole,
        out_shape=jax.ShapeDtypeStruct((tokens, WIDTH), jnp.bfloat16),
        scratch_shapes=[pltpu.VMEM((tokens, D), jnp.bfloat16)],
        compiler_params=params(16),
        cost_estimate=pl.CostEstimate(
            flops=2 * tokens * D * WIDTH, bytes_accessed=4_000_000, transcendentals=0
        ),
        name="project_queries",
    )(ids, *pieces, weight, gain)


def keys_kernel(steps, ids, *refs):
    pieces, (w_ref, gain_ref, out_ref, rows_ref) = refs[:HALF], refs[HALF:]
    gather_rows(ids, steps, pieces, rows_ref)
    rows = rows_ref[...]
    keys = jnp.dot(rows, w_ref[1], preferred_element_type=jnp.float32)
    out_ref[:, :WIDTH] = normed(keys, gain_ref[...])
    values = jnp.dot(rows, w_ref[2], preferred_element_type=jnp.float32)
    out_ref[:, WIDTH:] = values.astype(jnp.bfloat16)


def project_keys(steps, ids, pieces, weight, gain):
    tokens = HALF * PIECE
    whole = pl.BlockSpec(memory_space=pltpu.VMEM)
    return pl.pallas_call(
        functools.partial(keys_kernel, steps),
        in_specs=[pl.BlockSpec(memory_space=pltpu.SMEM)] + [whole] * (HALF + 2),
        out_specs=whole,
        out_shape=jax.ShapeDtypeStruct((tokens, 2 * WIDTH), jnp.bfloat16),
        scratch_shapes=[pltpu.VMEM((tokens, D), jnp.bfloat16)],
        compiler_params=params(16),
        cost_estimate=pl.CostEstimate(
            flops=2 * tokens * D * 2 * WIDTH, bytes_accessed=6_000_000, transcendentals=0
        ),
        name="project_keys",
    )(ids, *pieces, weight, gain)


TAIL = slice(TILE_COLS * PIECE, (TILE_COLS + 1) * PIECE)


def store_level(ref, level):
    for n in range(3):
        rounded = level.astype(jnp.bfloat16)
        level = level - rounded.astype(jnp.float32)
        ref[TAIL, n * HEAD_DIM : (n + 1) * HEAD_DIM] = rounded


def load_level(ref):
    parts = [ref[TAIL, n * HEAD_DIM : (n + 1) * HEAD_DIM].astype(jnp.float32) for n in range(3)]
    return parts[0] + (parts[1] + parts[2])


def merge(shares, out_ref):
    levels = [load_level(ref) for ref in shares]
    top = functools.reduce(jnp.maximum, levels)
    weights = [jnp.exp2(level - top) for level in levels]
    total = functools.reduce(jnp.add, weights)
    weights = [weight / total for weight in weights]
    for c in range(TILE_COLS):
        rows = slice(c * PIECE, (c + 1) * PIECE)
        for h in range(HEADS_HERE):
            head = slice(h * HEAD_DIM, (h + 1) * HEAD_DIM)
            lane = HEADS_HERE * c + h
            mixed = None
            for weight, ref in zip(weights, shares):
                term = weight[:, lane : lane + 1] * ref[rows, head].astype(jnp.float32)
                mixed = term if mixed is None else mixed + term
            out_ref[rows, head] = mixed.astype(jnp.bfloat16)
    return top + jnp.log2(total)


def merge_kernel(*refs):
    *shares, out_ref = refs
    store_level(out_ref, merge(shares, out_ref))


def merge_shares(*shares):
    whole = pl.BlockSpec(memory_space=pltpu.VMEM)
    return pl.pallas_call(
        merge_kernel,
        in_specs=[whole] * len(shares),
        out_specs=whole,
        out_shape=jax.ShapeDtypeStruct(shares[0].shape, shares[0].dtype),
        compiler_params=params(8),
        cost_estimate=pl.CostEstimate(flops=500_000, bytes_accessed=1_000_000, transcendentals=0),
        name="merge_shares",
    )(*shares)


def attend_kernel(kinds, table, *refs):
    count = len(kinds)
    refs = list(refs)
    take = lambda n: [refs.pop(0) for _ in range(n)]
    queries, halves = take(PLANE), take(2 * count)
    outs = take(PLANE)
    piece_of = lax.broadcasted_iota(jnp.int32, (1, count * WINDOW), 1) // PIECE
    ones = jnp.ones((count * WINDOW, HEAD_DIM), jnp.bfloat16)
    slots_ref = refs.pop(0)
    level_ref = refs.pop(0)
    size = HALF * PIECE
    for n in range(count):
        for e in range(2):
            start = pl.multiple_of((table[GROUP] // HALF ^ e) * size, size)
            slots_ref[n, pl.ds(start, size), :] = halves[2 * n + e][...]
    slots = [slots_ref.at[n] for n in range(count)]
    level_ref[...] = jnp.zeros_like(level_ref)
    for c in range(TILE_COLS):
        here = slice(c * PIECE, (c + 1) * PIECE)
        window = pl.ds(pl.multiple_of(table[STARTS + c] * PIECE, PIECE), WINDOW)
        bias = jnp.full((1, count * WINDOW), -jnp.inf, jnp.float32)
        for n in range(3 * count):
            bias = jnp.where((piece_of == n) & (table[FLAGS + 9 * c + kinds[n // 3] * 3 + n % 3] > 0), 0.0, bias)
        for h in range(HEADS_HERE):
            head = slice(h * HEAD_DIM, (h + 1) * HEAD_DIM)
            value_head = slice(WIDTH + h * HEAD_DIM, WIDTH + (h + 1) * HEAD_DIM)
            lane = slice(HEADS_HERE * c + h, HEADS_HERE * c + h + 1)
            q = jnp.concatenate([ref[here, head] for ref in queries], axis=0)
            k = jnp.concatenate([slot[window, head] for slot in slots], axis=0)
            v = jnp.concatenate([slot[window, value_head] for slot in slots], axis=0)
            scores = lax.dot_general(
                q, k, (((1,), (1,)), ((), ())), preferred_element_type=jnp.float32
            )
            scores = scores * SCORE_SCALE + bias
            top = jnp.maximum(jnp.max(scores, axis=-1, keepdims=True), LOWEST)
            weights = jnp.exp2(scores - top).astype(jnp.bfloat16)
            both = jnp.dot(
                weights, jnp.concatenate([v, ones], axis=1), preferred_element_type=jnp.float32
            )
            mixed, total = both[:, :HEAD_DIM], both[:, HEAD_DIM:]
            mixed = mixed / jnp.maximum(total, 0.5)
            level = jnp.maximum(top + jnp.log2(total), LOWEST)
            mixed = mixed.astype(jnp.bfloat16)
            for n in range(PLANE):
                outs[n][here, head] = mixed[n * PIECE : (n + 1) * PIECE]
            level_ref[:, lane] = level[:, lane]
    for n in range(PLANE):
        store_level(outs[n], level_ref[n * PIECE : (n + 1) * PIECE])


def attend(table, queries, slots, kinds):
    tokens = TILE_COLS * PIECE
    count = len(slots)
    whole = pl.BlockSpec(memory_space=pltpu.VMEM)
    scalars = pl.BlockSpec(memory_space=pltpu.SMEM)
    operands = [*queries, *(half for slot in slots for half in slot)]
    out_shape = [jax.ShapeDtypeStruct((tokens + PIECE, WIDTH), jnp.bfloat16)] * PLANE
    scratch = [
        pltpu.VMEM((count, tokens, 2 * WIDTH), jnp.bfloat16),
        pltpu.VMEM((PLANE * PIECE, HEAD_DIM), jnp.float32),
    ]
    return pl.pallas_call(
        functools.partial(attend_kernel, kinds),
        in_specs=[scalars] + [whole] * len(operands),
        out_specs=[whole] * len(out_shape),
        out_shape=out_shape,
        scratch_shapes=scratch,
        compiler_params=params(16),
        cost_estimate=pl.CostEstimate(
            flops=4 * PLANE * tokens * count * WINDOW * WIDTH,
            bytes_accessed=4_000_000,
            transcendentals=1_000_000,
        ),
        name="attend",
    )(table, *operands)


def term(ids, k, attended, w_ref, out_ref):
    columns = pl.ds(pl.multiple_of((ids[1] ^ k) * WIDTH, WIDTH), WIDTH)
    out_ref[...] = jnp.dot(
        attended, w_ref[:, columns], preferred_element_type=jnp.float32
    ).astype(jnp.bfloat16)


def join_kernel(ids, *refs):
    *shares, w_ref, joined = refs[: -len(RELAYED)]
    merge(shares, joined)
    for k, out_ref in zip(RELAYED, refs[-len(RELAYED) :]):
        term(ids, k, joined[...], w_ref, out_ref)


def join(ids, shares, w_out):
    tokens = TILE_COLS * PIECE
    whole = pl.BlockSpec(memory_space=pltpu.VMEM)
    return pl.pallas_call(
        join_kernel,
        in_specs=[pl.BlockSpec(memory_space=pltpu.SMEM)] + [whole] * (len(shares) + 1),
        out_specs=[whole] * (1 + len(RELAYED)),
        out_shape=[jax.ShapeDtypeStruct((tokens, WIDTH), jnp.bfloat16)] * (1 + len(RELAYED)),
        compiler_params=params(16),
        cost_estimate=pl.CostEstimate(
            flops=2 * tokens * WIDTH * WIDTH * len(RELAYED), bytes_accessed=3_000_000, transcendentals=0
        ),
        name="join",
    )(ids, *shares, w_out)


def terms_kernel(ids, joined, w_ref, *outs):
    for k, out_ref in zip(DIRECT, outs):
        term(ids, k, joined[...], w_ref, out_ref)


def direct_terms(ids, joined, w_out):
    whole = pl.BlockSpec(memory_space=pltpu.VMEM)
    return pl.pallas_call(
        terms_kernel,
        in_specs=[pl.BlockSpec(memory_space=pltpu.SMEM)] + [whole] * 2,
        out_specs=[whole] * len(DIRECT),
        out_shape=[jax.ShapeDtypeStruct(joined.shape, jnp.bfloat16)] * len(DIRECT),
        compiler_params=params(16),
        cost_estimate=pl.CostEstimate(
            flops=2 * joined.size * WIDTH * len(DIRECT), bytes_accessed=4_000_000, transcendentals=0
        ),
        name="direct_terms",
    )(ids, joined, w_out)


def add_kernel(table, *refs):
    *terms, kept_ref, given_ref, rows = refs
    total = terms[0][...].astype(jnp.float32)
    for ref in terms[1:]:
        total = total + ref[...].astype(jnp.float32)
    rows[...] = total.astype(jnp.bfloat16)
    for c in range(TILE_COLS):
        to = slice(c * PAIR, (c + 1) * PAIR)
        for ref, which in ((kept_ref, table[SIDE]), (given_ref, 1 - table[SIDE])):
            start = pl.multiple_of(c * PIECE + which * PAIR, PAIR)
            ref[to, :] = rows[pl.ds(start, PAIR), :]


def add_terms(table, terms):
    whole = pl.BlockSpec(memory_space=pltpu.VMEM)
    return pl.pallas_call(
        add_kernel,
        in_specs=[pl.BlockSpec(memory_space=pltpu.SMEM)] + [whole] * len(terms),
        out_specs=[whole] * 2,
        out_shape=[jax.ShapeDtypeStruct((TILE_COLS * PAIR, WIDTH), jnp.bfloat16)] * 2,
        scratch_shapes=[pltpu.VMEM((TILE_COLS * PIECE, WIDTH), jnp.bfloat16)],
        compiler_params=params(8),
        cost_estimate=pl.CostEstimate(flops=800_000, bytes_accessed=2_000_000, transcendentals=0),
        name="add_terms",
    )(table, *terms)


def order_kernel(table, kept_ref, got_ref, out_ref, rows):
    size = TILE_COLS * PAIR
    for ref, which in ((kept_ref, table[SIDE]), (got_ref, 1 - table[SIDE])):
        rows[pl.ds(pl.multiple_of(which * size, size), size), :] = ref[...]
    for d in range(TILES):
        start = pl.multiple_of((table[TILE_OF + d] % (2 * TILE_COLS)) * PAIR, PAIR)
        out_ref[d * PAIR : (d + 1) * PAIR, :] = rows[pl.ds(start, PAIR), :]


def order(table, kept, got):
    whole = pl.BlockSpec(memory_space=pltpu.VMEM)
    scalars = pl.BlockSpec(memory_space=pltpu.SMEM)
    return pl.pallas_call(
        order_kernel,
        in_specs=[scalars, whole, whole],
        out_specs=whole,
        out_shape=jax.ShapeDtypeStruct((TILES * PAIR, WIDTH), jnp.bfloat16),
        scratch_shapes=[pltpu.VMEM((2 * TILE_COLS * PAIR, WIDTH), jnp.bfloat16)],
        compiler_params=params(8),
        cost_estimate=pl.CostEstimate(flops=100_000, bytes_accessed=800_000, transcendentals=0),
        name="order",
    )(table, kept, got)


def tile_kernel(table, arrived, out_ref):
    base = table[FIRST] * (2 * TILE * PAIR)
    pieces = [
        arrived[pl.ds(pl.multiple_of(base + n * PAIR, PAIR), PAIR), :].astype(jnp.float32)
        for n in range(2 * TILE)
    ]
    parts = [
        pieces[(f // 2) * TILE + j][(f % 2) * TILE : (f % 2 + 1) * TILE]
        for f in range(FRAMES)
        for j in range(TILE)
    ]
    out_ref[...] = jnp.concatenate(parts, axis=0).astype(jnp.bfloat16)


def to_tile(table, arrived):
    whole = pl.BlockSpec(memory_space=pltpu.VMEM)
    return pl.pallas_call(
        tile_kernel,
        in_specs=[pl.BlockSpec(memory_space=pltpu.SMEM), whole],
        out_specs=whole,
        out_shape=jax.ShapeDtypeStruct((TILE_TOKENS, WIDTH), jnp.bfloat16),
        compiler_params=params(8),
        cost_estimate=pl.CostEstimate(flops=100_000, bytes_accessed=800_000, transcendentals=0),
        name="to_tile",
    )(table, arrived)


def head_swap(array, k):
    return lax.ppermute(array, "head", [(h, h ^ k) for h in range(N_HEAD)])


def plane_swap(array, k):
    return lax.ppermute(array, "seq", [(s, s ^ k) for s in range(PLANE * PLANES)])


def mate_swap(array):
    return plane_swap(array, PLANE)


def edge_swap(array):
    pairs = []
    for z in range(1, PLANES - 1, 2):
        for i in range(PLANE):
            pairs += [(z * PLANE + i, (z + 1) * PLANE + i), ((z + 1) * PLANE + i, z * PLANE + i)]
    return lax.ppermute(array, "seq", pairs)


def local(latent, w_qkv, q_gain, k_gain, w_out, neighbours, tile_owner):
    ids = jnp.stack([lax.axis_index("seq"), lax.axis_index("head")]).astype(jnp.int32)
    weight = load_weight(jnp.transpose(w_qkv, (1, 0, 2)))
    q_gain, k_gain = q_gain.reshape(1, HEAD_DIM), k_gain.reshape(1, HEAD_DIM)
    table = plan(ids, neighbours.T, tile_owner)

    pieces = [latent.reshape(PIECE, D)] * N_HEAD
    for k in (1, 2, 3, 6, 7):
        pieces[k] = head_swap(pieces[0], k)
    pieces[4], pieces[5] = head_swap(pieces[6], 2), head_swap(pieces[3], 6)

    own_a = project_keys(range(HALF), ids, pieces[:HALF], weight, k_gain)
    mate_a, edge_a = mate_swap(own_a), edge_swap(own_a)
    pieces_b, _own = lax.optimization_barrier((pieces[HALF:], own_a))
    own_b = project_keys(range(HALF, N_HEAD), ids, pieces_b, weight, k_gain)
    mate_b, edge_b = mate_swap(own_b), edge_swap(own_b)
    edge_2a, far_1a = edge_swap(mate_a), mate_swap(edge_a)

    queries = project_queries(ids, [*pieces[:HALF], *pieces_b], weight, q_gain)
    q_chip = plane_swap(queries, 2)
    all_queries = [queries, plane_swap(queries, 1), q_chip, plane_swap(q_chip, 1)]

    edge_b, edge_2a, all_queries = lax.optimization_barrier((edge_b, edge_2a, all_queries))
    edge_2b = edge_swap(mate_b)
    far_1b, far_2a = mate_swap(edge_b), mate_swap(edge_2a)
    far_2b = mate_swap(edge_2b)
    near_slots = [(_own, own_b), (mate_a, mate_b), (edge_a, edge_b)]
    far_slots = [(edge_2a, edge_2b), (far_1a, far_1b), (far_2a, far_2b)]
    near = attend(table, all_queries, near_slots, (0, 0, 1))
    near_own = merge_shares(near[0], plane_swap(near[1], 1))
    near_chip = merge_shares(near[2], plane_swap(near[3], 1))
    far = attend(table, all_queries, far_slots, (1, 2, 2))
    from_core, for_chip = plane_swap(far[1], 1), plane_swap(far[3], 1)
    from_chip = plane_swap(merge_shares(near_chip, far[2], for_chip), 2)

    joined, *relayed = join(ids, [near_own, far[0], from_core, from_chip], w_out)
    passed = {6: head_swap(relayed[0], 2), 3: head_swap(relayed[1], 6)}
    terms = dict(zip(DIRECT, direct_terms(ids, joined, w_out)))
    for k in (6, 3):
        terms[k] = (terms[k].astype(jnp.float32) + passed[k].astype(jnp.float32)).astype(jnp.bfloat16)
    terms = [terms[0]] + [head_swap(terms[k], k) for k in DIRECT[1:]]

    kept, given = add_terms(table, terms)
    sent = order(table, kept, plane_swap(given, TILE))
    arrived = lax.all_to_all(
        sent.reshape(TILES, PAIR, WIDTH), "seq", split_axis=0, concat_axis=0, tiled=True
    )
    return to_tile(table, arrived.reshape(TILES * PAIR, WIDTH)).reshape(1, TILE_TOKENS, WIDTH)


def solution(mesh):
    placed = (
        P(None, "seq", "head", None),
        P(None, None, "head"),
        P(),
        P(),
        P("head", None),
        P(),
        P(),
    )
    return jax.shard_map(
        local, mesh=mesh, in_specs=placed, out_specs=P("seq", None, "head"), check_vma=False
    )
```

```python
import functools

import jax
import jax.numpy as jnp
from jax import lax
from jax.experimental import pallas as pl
from jax.experimental.pallas import tpu as pltpu
from jax.sharding import PartitionSpec as P

D = 3072
HEAD_DIM = 128
FRAMES = 4
TILE = 8
TILE_COLS = 8
TILES = 32
TILE_TOKENS = 256
N_HEAD = 8
PLANE = 4
PLANES = 8
PIECE = FRAMES * TILE
PAIR = 2 * TILE
WIDTH = 384
HEADS_HERE = 3
SLOTS = 6
WINDOW = 3 * PIECE
HALF = N_HEAD // 2
SCORE_SCALE = HEAD_DIM ** (-0.5) * 1.4426950408889634

LOADS = 4

RELAYED = (4, 5)
DIRECT = (0, 1, 2, 7, 6, 3)

epsilon = 1e-06
LOWEST = -1e30


def params(mib):
    return pltpu.CompilerParams(vmem_limit_bytes=mib * 1024 * 1024)


STARTS, FLAGS, TILE_OF, FIRST, SIDE, GROUP = 0, 8, 80, 112, 113, 114


def plan_kernel(ids, neighbours, tile_owner, table):
    position = ids[0]
    tile_row = position // TILE
    odd = (position // PLANE) % 2
    for c in range(TILE_COLS):
        tile = tile_row * TILE_COLS + c
        start = jnp.minimum(neighbours[0, tile] % TILE_COLS, TILE_COLS - 3)
        table[STARTS + c] = start
        for n in range(9):
            table[FLAGS + 9 * c + n] = 0
        for n in range(9):
            listed = neighbours[n, tile]

            @pl.when(listed >= 0)
            def _():
                step = listed // TILE_COLS - tile_row
                kind = jnp.where(step == 0, 0, jnp.where((step > 0) == (odd == 1), 1, 2))
                table[FLAGS + 9 * c + kind * 3 + listed % TILE_COLS - start] = 1

    for t in range(TILES):
        table[TILE_OF + tile_owner[t]] = t
    table[FIRST] = table[TILE_OF + position] // (2 * TILE_COLS)
    table[SIDE] = tile_row % 2
    table[GROUP] = ids[1]


def plan(ids, neighbours, tile_owner):
    scalars = pl.BlockSpec(memory_space=pltpu.SMEM)
    return pl.pallas_call(
        plan_kernel,
        in_specs=[scalars] * 3,
        out_specs=scalars,
        out_shape=jax.ShapeDtypeStruct((128,), jnp.int32),
        compiler_params=params(8),
        cost_estimate=pl.CostEstimate(flops=0, bytes_accessed=8_000_000, transcendentals=0),
        name="plan",
    )(ids, neighbours, tile_owner)


def normed(result, gain):
    heads = []
    for h in range(HEADS_HERE):
        part = result[:, h * HEAD_DIM : (h + 1) * HEAD_DIM]
        mean = jnp.mean(part * part, axis=-1, keepdims=True)
        heads.append((part * lax.rsqrt(mean + epsilon) * gain).astype(jnp.bfloat16))
    return jnp.concatenate(heads, axis=1)


def gather_rows(ids, steps, pieces, rows):
    count = len(pieces)
    for k, piece in zip(steps, pieces):
        start = pl.multiple_of(((ids[1] ^ k) % count) * PIECE, PIECE)
        rows[pl.ds(start, PIECE), :] = piece[...]


def load_kernel(parts, w_ref, out_ref, sems):
    rows = D // LOADS
    copies = []
    for n, part in enumerate(parts):
        for e in range(LOADS):
            some = pl.ds(e * rows, rows)
            copies.append(
                pltpu.make_async_copy(w_ref.at[part, some], out_ref.at[n, some], sems.at[n, e])
            )
    for copy in copies:
        copy.start()
    for copy in copies:
        copy.wait()


def load_weight(weight, parts, mib):
    return pl.pallas_call(
        functools.partial(load_kernel, parts),
        in_specs=[pl.BlockSpec(memory_space=pltpu.HBM)],
        out_specs=pl.BlockSpec(memory_space=pltpu.VMEM),
        out_shape=jax.ShapeDtypeStruct((len(parts),) + weight.shape[1:], weight.dtype),
        scratch_shapes=[pltpu.SemaphoreType.DMA((len(parts), LOADS))],
        compiler_params=params(mib),
        cost_estimate=pl.CostEstimate(
            flops=0, bytes_accessed=2_400_000 * len(parts), transcendentals=0
        ),
        name="load_weight",
    )(weight)


def queries_kernel(ids, *refs):
    pieces, (w_ref, gain_ref, out_ref, rows_ref) = refs[:N_HEAD], refs[N_HEAD:]
    gather_rows(ids, range(N_HEAD), pieces, rows_ref)
    result = jnp.dot(rows_ref[...], w_ref[0], preferred_element_type=jnp.float32)
    out_ref[...] = normed(result, gain_ref[...])


def project_queries(ids, pieces, weight, gain):
    tokens = N_HEAD * PIECE
    whole = pl.BlockSpec(memory_space=pltpu.VMEM)
    return pl.pallas_call(
        queries_kernel,
        in_specs=[pl.BlockSpec(memory_space=pltpu.SMEM)] + [whole] * (N_HEAD + 2),
        out_specs=whole,
        out_shape=jax.ShapeDtypeStruct((tokens, WIDTH), jnp.bfloat16),
        scratch_shapes=[pltpu.VMEM((tokens, D), jnp.bfloat16)],
        compiler_params=params(16),
        cost_estimate=pl.CostEstimate(
            flops=2 * tokens * D * WIDTH, bytes_accessed=4_000_000, transcendentals=0
        ),
        name="project_queries",
    )(ids, *pieces, weight, gain)


def keys_kernel(steps, ids, *refs):
    pieces, (w_ref, gain_ref, out_ref, rows_ref) = refs[:HALF], refs[HALF:]
    gather_rows(ids, steps, pieces, rows_ref)
    rows = rows_ref[...]
    keys = jnp.dot(rows, w_ref[0], preferred_element_type=jnp.float32)
    out_ref[:, :WIDTH] = normed(keys, gain_ref[...])
    values = jnp.dot(rows, w_ref[1], preferred_element_type=jnp.float32)
    out_ref[:, WIDTH:] = values.astype(jnp.bfloat16)


def project_keys(steps, ids, pieces, weight, gain):
    tokens = HALF * PIECE
    whole = pl.BlockSpec(memory_space=pltpu.VMEM)
    return pl.pallas_call(
        functools.partial(keys_kernel, steps),
        in_specs=[pl.BlockSpec(memory_space=pltpu.SMEM)] + [whole] * (HALF + 2),
        out_specs=whole,
        out_shape=jax.ShapeDtypeStruct((tokens, 2 * WIDTH), jnp.bfloat16),
        scratch_shapes=[pltpu.VMEM((tokens, D), jnp.bfloat16)],
        compiler_params=params(16),
        cost_estimate=pl.CostEstimate(
            flops=2 * tokens * D * 2 * WIDTH, bytes_accessed=6_000_000, transcendentals=0
        ),
        name="project_keys",
    )(ids, *pieces, weight, gain)


TAIL = slice(TILE_COLS * PIECE, (TILE_COLS + 1) * PIECE)


def store_level(ref, level):
    for n in range(3):
        rounded = level.astype(jnp.bfloat16)
        level = level - rounded.astype(jnp.float32)
        ref[TAIL, n * HEAD_DIM : (n + 1) * HEAD_DIM] = rounded


def load_level(ref):
    parts = [ref[TAIL, n * HEAD_DIM : (n + 1) * HEAD_DIM].astype(jnp.float32) for n in range(3)]
    return parts[0] + (parts[1] + parts[2])


def merge(shares, out_ref):
    levels = [load_level(ref) for ref in shares]
    top = functools.reduce(jnp.maximum, levels)
    weights = [jnp.exp2(level - top) for level in levels]
    total = functools.reduce(jnp.add, weights)
    weights = [weight / total for weight in weights]
    for c in range(TILE_COLS):
        rows = slice(c * PIECE, (c + 1) * PIECE)
        for h in range(HEADS_HERE):
            head = slice(h * HEAD_DIM, (h + 1) * HEAD_DIM)
            lane = HEADS_HERE * c + h
            mixed = None
            for weight, ref in zip(weights, shares):
                term = weight[:, lane : lane + 1] * ref[rows, head].astype(jnp.float32)
                mixed = term if mixed is None else mixed + term
            out_ref[rows, head] = mixed.astype(jnp.bfloat16)
    return top + jnp.log2(total)


def merge_kernel(*refs):
    *shares, out_ref = refs
    store_level(out_ref, merge(shares, out_ref))


def merge_shares(*shares):
    whole = pl.BlockSpec(memory_space=pltpu.VMEM)
    return pl.pallas_call(
        merge_kernel,
        in_specs=[whole] * len(shares),
        out_specs=whole,
        out_shape=jax.ShapeDtypeStruct(shares[0].shape, shares[0].dtype),
        compiler_params=params(8),
        cost_estimate=pl.CostEstimate(flops=500_000, bytes_accessed=1_000_000, transcendentals=0),
        name="merge_shares",
    )(*shares)


def attend_kernel(kinds, table, *refs):
    count = len(kinds)
    refs = list(refs)
    take = lambda n: [refs.pop(0) for _ in range(n)]
    queries, halves = take(PLANE), take(2 * count)
    outs = take(PLANE)
    piece_of = lax.broadcasted_iota(jnp.int32, (1, count * WINDOW), 1) // PIECE
    ones = jnp.ones((count * WINDOW, HEAD_DIM), jnp.bfloat16)
    slots_ref = refs.pop(0)
    level_ref = refs.pop(0)
    size = HALF * PIECE
    for n in range(count):
        for e in range(2):
            start = pl.multiple_of((table[GROUP] // HALF ^ e) * size, size)
            slots_ref[n, pl.ds(start, size), :] = halves[2 * n + e][...]
    slots = [slots_ref.at[n] for n in range(count)]
    level_ref[...] = jnp.zeros_like(level_ref)
    for c in range(TILE_COLS):
        here = slice(c * PIECE, (c + 1) * PIECE)
        window = pl.ds(pl.multiple_of(table[STARTS + c] * PIECE, PIECE), WINDOW)
        bias = jnp.full((1, count * WINDOW), -jnp.inf, jnp.float32)
        for n in range(3 * count):
            bias = jnp.where((piece_of == n) & (table[FLAGS + 9 * c + kinds[n // 3] * 3 + n % 3] > 0), 0.0, bias)
        for h in range(HEADS_HERE):
            head = slice(h * HEAD_DIM, (h + 1) * HEAD_DIM)
            value_head = slice(WIDTH + h * HEAD_DIM, WIDTH + (h + 1) * HEAD_DIM)
            lane = slice(HEADS_HERE * c + h, HEADS_HERE * c + h + 1)
            q = jnp.concatenate([ref[here, head] for ref in queries], axis=0)
            k = jnp.concatenate([slot[window, head] for slot in slots], axis=0)
            v = jnp.concatenate([slot[window, value_head] for slot in slots], axis=0)
            scores = lax.dot_general(
                q, k, (((1,), (1,)), ((), ())), preferred_element_type=jnp.float32
            )
            scores = scores * SCORE_SCALE + bias
            top = jnp.maximum(jnp.max(scores, axis=-1, keepdims=True), LOWEST)
            weights = jnp.exp2(scores - top).astype(jnp.bfloat16)
            both = jnp.dot(
                weights, jnp.concatenate([v, ones], axis=1), preferred_element_type=jnp.float32
            )
            mixed, total = both[:, :HEAD_DIM], both[:, HEAD_DIM:]
            mixed = mixed / jnp.maximum(total, 0.5)
            level = jnp.maximum(top + jnp.log2(total), LOWEST)
            mixed = mixed.astype(jnp.bfloat16)
            for n in range(PLANE):
                outs[n][here, head] = mixed[n * PIECE : (n + 1) * PIECE]
            level_ref[:, lane] = level[:, lane]
    for n in range(PLANE):
        store_level(outs[n], level_ref[n * PIECE : (n + 1) * PIECE])


def attend(table, queries, slots, kinds):
    tokens = TILE_COLS * PIECE
    count = len(slots)
    whole = pl.BlockSpec(memory_space=pltpu.VMEM)
    scalars = pl.BlockSpec(memory_space=pltpu.SMEM)
    operands = [*queries, *(half for slot in slots for half in slot)]
    out_shape = [jax.ShapeDtypeStruct((tokens + PIECE, WIDTH), jnp.bfloat16)] * PLANE
    scratch = [
        pltpu.VMEM((count, tokens, 2 * WIDTH), jnp.bfloat16),
        pltpu.VMEM((PLANE * PIECE, HEAD_DIM), jnp.float32),
    ]
    return pl.pallas_call(
        functools.partial(attend_kernel, kinds),
        in_specs=[scalars] + [whole] * len(operands),
        out_specs=[whole] * len(out_shape),
        out_shape=out_shape,
        scratch_shapes=scratch,
        compiler_params=params(16),
        cost_estimate=pl.CostEstimate(
            flops=4 * PLANE * tokens * count * WINDOW * WIDTH,
            bytes_accessed=4_000_000,
            transcendentals=1_000_000,
        ),
        name="attend",
    )(table, *operands)


def term(ids, k, attended, w_ref, out_ref):
    columns = pl.ds(pl.multiple_of((ids[1] ^ k) * WIDTH, WIDTH), WIDTH)
    out_ref[...] = jnp.dot(
        attended, w_ref[:, columns], preferred_element_type=jnp.float32
    ).astype(jnp.bfloat16)


def join_kernel(ids, *refs):
    *shares, w_ref, joined = refs[: -len(RELAYED)]
    merge(shares, joined)
    for k, out_ref in zip(RELAYED, refs[-len(RELAYED) :]):
        term(ids, k, joined[...], w_ref, out_ref)


def join(ids, shares, w_out):
    tokens = TILE_COLS * PIECE
    whole = pl.BlockSpec(memory_space=pltpu.VMEM)
    return pl.pallas_call(
        join_kernel,
        in_specs=[pl.BlockSpec(memory_space=pltpu.SMEM)] + [whole] * (len(shares) + 1),
        out_specs=[whole] * (1 + len(RELAYED)),
        out_shape=[jax.ShapeDtypeStruct((tokens, WIDTH), jnp.bfloat16)] * (1 + len(RELAYED)),
        compiler_params=params(16),
        cost_estimate=pl.CostEstimate(
            flops=2 * tokens * WIDTH * WIDTH * len(RELAYED), bytes_accessed=3_000_000, transcendentals=0
        ),
        name="join",
    )(ids, *shares, w_out)


def terms_kernel(ids, joined, w_ref, *outs):
    for k, out_ref in zip(DIRECT, outs):
        term(ids, k, joined[...], w_ref, out_ref)


def direct_terms(ids, joined, w_out):
    whole = pl.BlockSpec(memory_space=pltpu.VMEM)
    return pl.pallas_call(
        terms_kernel,
        in_specs=[pl.BlockSpec(memory_space=pltpu.SMEM)] + [whole] * 2,
        out_specs=[whole] * len(DIRECT),
        out_shape=[jax.ShapeDtypeStruct(joined.shape, jnp.bfloat16)] * len(DIRECT),
        compiler_params=params(16),
        cost_estimate=pl.CostEstimate(
            flops=2 * joined.size * WIDTH * len(DIRECT), bytes_accessed=4_000_000, transcendentals=0
        ),
        name="direct_terms",
    )(ids, joined, w_out)


def add_kernel(table, *refs):
    *terms, kept_ref, given_ref, rows = refs
    total = terms[0][...].astype(jnp.float32)
    for ref in terms[1:]:
        total = total + ref[...].astype(jnp.float32)
    rows[...] = total.astype(jnp.bfloat16)
    for c in range(TILE_COLS):
        to = slice(c * PAIR, (c + 1) * PAIR)
        for ref, which in ((kept_ref, table[SIDE]), (given_ref, 1 - table[SIDE])):
            start = pl.multiple_of(c * PIECE + which * PAIR, PAIR)
            ref[to, :] = rows[pl.ds(start, PAIR), :]


def add_terms(table, terms):
    whole = pl.BlockSpec(memory_space=pltpu.VMEM)
    return pl.pallas_call(
        add_kernel,
        in_specs=[pl.BlockSpec(memory_space=pltpu.SMEM)] + [whole] * len(terms),
        out_specs=[whole] * 2,
        out_shape=[jax.ShapeDtypeStruct((TILE_COLS * PAIR, WIDTH), jnp.bfloat16)] * 2,
        scratch_shapes=[pltpu.VMEM((TILE_COLS * PIECE, WIDTH), jnp.bfloat16)],
        compiler_params=params(8),
        cost_estimate=pl.CostEstimate(flops=800_000, bytes_accessed=2_000_000, transcendentals=0),
        name="add_terms",
    )(table, *terms)


def order_kernel(table, kept_ref, got_ref, out_ref, rows):
    size = TILE_COLS * PAIR
    for ref, which in ((kept_ref, table[SIDE]), (got_ref, 1 - table[SIDE])):
        rows[pl.ds(pl.multiple_of(which * size, size), size), :] = ref[...]
    for d in range(TILES):
        start = pl.multiple_of((table[TILE_OF + d] % (2 * TILE_COLS)) * PAIR, PAIR)
        out_ref[d * PAIR : (d + 1) * PAIR, :] = rows[pl.ds(start, PAIR), :]


def order(table, kept, got):
    whole = pl.BlockSpec(memory_space=pltpu.VMEM)
    scalars = pl.BlockSpec(memory_space=pltpu.SMEM)
    return pl.pallas_call(
        order_kernel,
        in_specs=[scalars, whole, whole],
        out_specs=whole,
        out_shape=jax.ShapeDtypeStruct((TILES * PAIR, WIDTH), jnp.bfloat16),
        scratch_shapes=[pltpu.VMEM((2 * TILE_COLS * PAIR, WIDTH), jnp.bfloat16)],
        compiler_params=params(8),
        cost_estimate=pl.CostEstimate(flops=100_000, bytes_accessed=800_000, transcendentals=0),
        name="order",
    )(table, kept, got)


def tile_kernel(table, arrived, out_ref):
    base = table[FIRST] * (2 * TILE * PAIR)
    pieces = [
        arrived[pl.ds(pl.multiple_of(base + n * PAIR, PAIR), PAIR), :].astype(jnp.float32)
        for n in range(2 * TILE)
    ]
    parts = [
        pieces[(f // 2) * TILE + j][(f % 2) * TILE : (f % 2 + 1) * TILE]
        for f in range(FRAMES)
        for j in range(TILE)
    ]
    out_ref[...] = jnp.concatenate(parts, axis=0).astype(jnp.bfloat16)


def to_tile(table, arrived):
    whole = pl.BlockSpec(memory_space=pltpu.VMEM)
    return pl.pallas_call(
        tile_kernel,
        in_specs=[pl.BlockSpec(memory_space=pltpu.SMEM), whole],
        out_specs=whole,
        out_shape=jax.ShapeDtypeStruct((TILE_TOKENS, WIDTH), jnp.bfloat16),
        compiler_params=params(8),
        cost_estimate=pl.CostEstimate(flops=100_000, bytes_accessed=800_000, transcendentals=0),
        name="to_tile",
    )(table, arrived)


def head_swap(array, k):
    return lax.ppermute(array, "head", [(h, h ^ k) for h in range(N_HEAD)])


def plane_swap(array, k):
    return lax.ppermute(array, "seq", [(s, s ^ k) for s in range(PLANE * PLANES)])


def mate_swap(array):
    return plane_swap(array, PLANE)


def edge_swap(array):
    pairs = []
    for z in range(1, PLANES - 1, 2):
        for i in range(PLANE):
            pairs += [(z * PLANE + i, (z + 1) * PLANE + i), ((z + 1) * PLANE + i, z * PLANE + i)]
    return lax.ppermute(array, "seq", pairs)


def local(latent, w_qkv, q_gain, k_gain, w_out, neighbours, tile_owner):
    ids = jnp.stack([lax.axis_index("seq"), lax.axis_index("head")]).astype(jnp.int32)
    weight = jnp.transpose(w_qkv, (1, 0, 2))
    kv_weight = load_weight(weight, (1, 2), 50)
    q_gain, k_gain = q_gain.reshape(1, HEAD_DIM), k_gain.reshape(1, HEAD_DIM)
    table = plan(ids, neighbours.T, tile_owner)

    pieces = [latent.reshape(PIECE, D)] * N_HEAD
    for k in (1, 2, 3, 6, 7):
        pieces[k] = head_swap(pieces[0], k)
    pieces[4], pieces[5] = head_swap(pieces[6], 2), head_swap(pieces[3], 6)

    own_a = project_keys(range(HALF), ids, pieces[:HALF], kv_weight, k_gain)
    mate_a, edge_a = mate_swap(own_a), edge_swap(own_a)
    pieces_b, _own = lax.optimization_barrier((pieces[HALF:], own_a))
    own_b = project_keys(range(HALF, N_HEAD), ids, pieces_b, kv_weight, k_gain)
    mate_b, edge_b = mate_swap(own_b), edge_swap(own_b)
    edge_2a, far_1a = edge_swap(mate_a), mate_swap(edge_a)

    queries = project_queries(ids, [*pieces[:HALF], *pieces_b], load_weight(weight, (0,), 49), q_gain)
    q_chip = plane_swap(queries, 2)
    all_queries = [queries, plane_swap(queries, 1), q_chip, plane_swap(q_chip, 1)]

    edge_b, edge_2a, all_queries = lax.optimization_barrier((edge_b, edge_2a, all_queries))
    edge_2b = edge_swap(mate_b)
    far_1b, far_2a = mate_swap(edge_b), mate_swap(edge_2a)
    far_2b = mate_swap(edge_2b)
    near_slots = [(_own, own_b), (mate_a, mate_b), (edge_a, edge_b)]
    far_slots = [(edge_2a, edge_2b), (far_1a, far_1b), (far_2a, far_2b)]
    near = attend(table, all_queries, near_slots, (0, 0, 1))
    near_own = merge_shares(near[0], plane_swap(near[1], 1))
    near_chip = merge_shares(near[2], plane_swap(near[3], 1))
    far = attend(table, all_queries, far_slots, (1, 2, 2))
    from_core, for_chip = plane_swap(far[1], 1), plane_swap(far[3], 1)
    from_chip = plane_swap(merge_shares(near_chip, far[2], for_chip), 2)

    joined, *relayed = join(ids, [near_own, far[0], from_core, from_chip], w_out)
    passed = {6: head_swap(relayed[0], 2), 3: head_swap(relayed[1], 6)}
    terms = dict(zip(DIRECT, direct_terms(ids, joined, w_out)))
    for k in (6, 3):
        terms[k] = (terms[k].astype(jnp.float32) + passed[k].astype(jnp.float32)).astype(jnp.bfloat16)
    terms = [terms[0]] + [head_swap(terms[k], k) for k in DIRECT[1:]]

    kept, given = add_terms(table, terms)
    sent = order(table, kept, plane_swap(given, TILE))
    arrived = lax.all_to_all(
        sent.reshape(TILES, PAIR, WIDTH), "seq", split_axis=0, concat_axis=0, tiled=True
    )
    return to_tile(table, arrived.reshape(TILES * PAIR, WIDTH)).reshape(1, TILE_TOKENS, WIDTH)


def solution(mesh):
    placed = (
        P(None, "seq", "head", None),
        P(None, None, "head"),
        P(),
        P(),
        P("head", None),
        P(),
        P(),
    )
    return jax.shard_map(
        local, mesh=mesh, in_specs=placed, out_specs=P("seq", None, "head"), check_vma=False
    )
```
